128 devices in a mesh: frame: 8 (over z_lo, y), tile: 16 (over x, z_hi, core).
Axes of the slice: x: 4, y: 4, z: 4 (z_hi: 2, z_lo: 2; z = z_hi * 2 + z_lo), core: 2. Of those that a mesh axis runs over, the one named last changes fastest.
Arguments:
- latent: bfloat16 [8, 64, 160, 384], P('frame', 'tile'), may hold values from -128 to 128
- norm1_gain: bfloat16 [384], replicated, may hold values from 0.5 to 2
- conv1_weight: bfloat16 [3, 3, 3, 384, 384], replicated, may hold values from -0.0625 to 0.0625
- norm2_gain: bfloat16 [384], replicated, may hold values from 0.5 to 2
- conv2_weight: bfloat16 [3, 3, 3, 384, 384], replicated, may hold values from -0.0625 to 0.0625
- attn_gain: bfloat16 [384], replicated, may hold values from 0.5 to 2
- query_weight: bfloat16 [384, 384], replicated, may hold values from -1 to 1
- key_weight: bfloat16 [384, 384], replicated, may hold values from -1 to 1
- value_weight: bfloat16 [384, 384], replicated, may hold values from -0.3125 to 0.3125
- out_weight: bfloat16 [384, 384], replicated, may hold values from -0.3125 to 0.3125
Outputs:
- decoded: bfloat16 [8, 64, 160, 384], P('frame', 'tile')
The draws below stay inside these ranges and needn't reach their ends.
All inputs are finite; a program needn't handle non-finite values.
Results may differ from the reference program's by a relative error of at most 0.025.
Values may be sent and summed in bfloat16 or wider, within the bound.
No kernel may reach another device: no remote copies, remote signals or barrier semaphores. Data moves between devices by JAX's collectives and lax.ppermute only.
A program may use at most 128 MiB of HBM per device.

```python
import math
import jax
import jax.numpy as jnp
from jax import lax

C = 384
W = 160
FRAMES = 8
H = 64


def draw_query_weight(key, part):
    key = jax.random.fold_in(key, 1)
    base_weight = jnp.clip(jax.random.normal(key, (C, C), jnp.float32), -4.0, 4.0) * (2.5 / math.sqrt(C))
    base_weight = jnp.clip(base_weight, -1.0, 1.0)
    return base_weight.astype(jnp.bfloat16)


def draw_key_weight(key, part):
    key = jax.random.fold_in(key, 2)
    base_weight = jnp.clip(jax.random.normal(key, (C, C), jnp.float32), -4.0, 4.0) * (1.0 / math.sqrt(C))
    base_weight = jnp.clip(base_weight, -1.0, 1.0)
    return base_weight.astype(jnp.bfloat16)


def draw_latent(key, part):
    key = jax.random.fold_in(key, 3)
    noise_key = jax.random.fold_in(key, 11)
    rough_key = jax.random.fold_in(key, 12)
    time_pos = jnp.arange(FRAMES).astype(jnp.float32) / max(FRAMES - 1, 1)
    row_pos = jnp.arange(H).astype(jnp.float32) / max(H - 1, 1)
    trend_scale = jnp.exp(math.log(3.0) * (time_pos[:, None, None, None] + row_pos[None, :, None, None]))
    noise_field = jnp.clip(jax.random.normal(noise_key, (FRAMES, H, W, C), jnp.float32), -4.0, 4.0)
    roughness = jnp.exp(jax.random.uniform(rough_key, (FRAMES, H, W, 1), jnp.float32, -0.5, 0.5))
    field = noise_field * trend_scale * roughness
    return field.astype(jnp.bfloat16)


def bell_draw(own_key, extent, width, bound, held_as=jnp.bfloat16):
    entries = jax.random.normal(own_key, extent, jnp.float32) * width
    return jnp.minimum(jnp.maximum(entries, -bound), bound).astype(held_as)


def setup_inputs(seed: int = 0) -> dict:
    arg_keys = jax.random.split(jax.random.key(seed), 11)
    return {
        "latent": draw_latent(jax.random.fold_in(arg_keys[10], 71), 0),
        "norm1_gain": jnp.clip(jnp.exp(jax.random.uniform(arg_keys[1], (C,), jnp.float32, math.log(0.5), math.log(2.0))), 0.5, 2.0).astype(jnp.bfloat16),
        "conv1_weight": bell_draw(arg_keys[2], (3, 3, 3, C, C), (27 * C) ** -0.5, 0.0625),
        "norm2_gain": jnp.clip(jnp.exp(jax.random.uniform(arg_keys[3], (C,), jnp.float32, math.log(0.5), math.log(2.0))), 0.5, 2.0).astype(jnp.bfloat16),
        "conv2_weight": bell_draw(arg_keys[4], (3, 3, 3, C, C), (27 * C) ** -0.5, 0.0625),
        "attn_gain": jnp.clip(jnp.exp(jax.random.uniform(arg_keys[5], (C,), jnp.float32, math.log(0.5), math.log(2.0))), 0.5, 2.0).astype(jnp.bfloat16),
        "query_weight": draw_query_weight(jax.random.fold_in(arg_keys[10], 71), 0),
        "key_weight": draw_key_weight(jax.random.fold_in(arg_keys[10], 71), 0),
        "value_weight": bell_draw(arg_keys[8], (C, C), C ** -0.5, 0.3125),
        "out_weight": bell_draw(arg_keys[9], (C, C), C ** -0.5, 0.3125),
    }


def norm_gain(field, gain):
    squares = lax.optimization_barrier(jnp.mean(field * field, axis=-1, keepdims=True))
    return field * lax.rsqrt(squares + 1e-06) * gain.astype(jnp.float32)

def norm_silu(field, gain):
    return jax.nn.silu(norm_gain(field, gain)).astype(jnp.bfloat16)

def convolve(activation, weight):
    frames, row_count, col_count, channels = activation.shape
    padded = jnp.pad(activation, ((2, 0), (1, 1), (1, 1), (0, 0)))
    running = jnp.zeros((frames * row_count * col_count, weight.shape[-1]), jnp.float32)
    for time_tap in range(3):
        for row_tap in range(3):
            portion = padded[time_tap:time_tap + frames, row_tap:row_tap + row_count]
            stacked = jnp.concatenate([portion[:, :, 0:col_count], portion[:, :, 1:col_count + 1], portion[:, :, 2:col_count + 2]], -1)
            running = running + jnp.dot(stacked.reshape(-1, 3 * channels), weight[time_tap, row_tap].reshape(3 * channels, -1), preferred_element_type=jnp.float32)
    return running.reshape(frames, row_count, col_count, -1)

def attend_frame(inputs):
    queries, key_rows, value_rows = inputs
    scores = jnp.dot(queries, key_rows.T, preferred_element_type=jnp.float32) * (1.0 / math.sqrt(C))
    ceiling = lax.optimization_barrier(jnp.max(scores, axis=-1, keepdims=True))
    weights = jnp.exp(scores - ceiling)
    summed = lax.optimization_barrier(jnp.sum(weights, axis=-1, keepdims=True))
    mixed = jnp.dot(weights.astype(jnp.bfloat16), value_rows, preferred_element_type=jnp.float32)
    return (mixed / summed).astype(jnp.bfloat16)

def project(normed, weight):
    flat_rows = jnp.dot(normed.reshape(-1, C), weight, preferred_element_type=jnp.float32)
    return flat_rows.astype(jnp.bfloat16).reshape(FRAMES, H * W, C)

def reference(latent, norm1_gain, conv1_weight, norm2_gain, conv2_weight, attn_gain, query_weight, key_weight, value_weight, out_weight):
    act_one = norm_silu(latent.astype(jnp.float32), norm1_gain)
    conv_one = convolve(act_one, conv1_weight).astype(jnp.bfloat16)
    act_two = norm_silu(conv_one.astype(jnp.float32), norm2_gain)
    hstate = (latent.astype(jnp.float32) + convolve(act_two, conv2_weight)).astype(jnp.bfloat16)
    flat_state = hstate.astype(jnp.float32).reshape(FRAMES, H * W, C)
    normed = norm_gain(flat_state, attn_gain).astype(jnp.bfloat16)
    queries = project(normed, query_weight)
    key_rows = project(normed, key_weight)
    value_rows = project(normed, value_weight)
    attended = lax.map(attend_frame, (queries, key_rows, value_rows))
    mixed = jnp.dot(attended.reshape(-1, C), out_weight, preferred_element_type=jnp.float32).reshape(FRAMES, H * W, C)
    return (flat_state + mixed).reshape(FRAMES, H, W, C).astype(jnp.bfloat16)
```

```python
import functools
import math

import jax
import jax.numpy as jnp
from jax import lax
from jax.experimental import pallas as pl
from jax.experimental.pallas import tpu as pltpu
from jax.sharding import PartitionSpec as P

C = 384
FRAMES = 8
ROWS = 4
COLS = 160
OWN = COLS // FRAMES
WIDE = OWN + 4
POS = ROWS * OWN
BOTH = ("frame", "tile")
VMEM = pl.BlockSpec(memory_space=pltpu.VMEM)
PARAMS = pltpu.CompilerParams(vmem_limit_bytes=48 * 2**20)
ROW_DOT = (((1,), (1,)), ((), ()))


def coords(device):
    frame, tile = divmod(device, 16)
    return frame, tile // 4, tile // 2 % 2, tile % 2


def permutation(move):
    pairs = []
    for device in range(128):
        frame, x, z, core = move(*coords(device))
        pairs.append((device, frame * 16 + x % 4 * 4 + z % 2 * 2 + core % 2))
    return pairs


CORE = permutation(lambda f, x, z, c: (f, x, z, c + 1))
UP_X = permutation(lambda f, x, z, c: (f, x + 1, z, c))
DOWN_X = permutation(lambda f, x, z, c: (f, x - 1, z, c))
OTHER_Z = permutation(lambda f, x, z, c: (f, x, z + 1, c))


def send(value, pairs):
    return lax.ppermute(value, BOTH, pairs)


def norm_gain(field, gain):
    squares = jnp.mean(field * field, axis=-1, keepdims=True)
    return field * lax.rsqrt(squares + 1e-06) * gain.astype(jnp.float32)


def silu(u):
    return u / (1.0 + jnp.exp(-u))


def pack_kernel(latent_ref, out_ref, field):
    field[:, 0:8, :] = jnp.zeros((ROWS, 8, C), jnp.float32)
    field[:, COLS + 8 : COLS + 16, :] = jnp.zeros((ROWS, 8, C), jnp.float32)
    field[:, 8 : COLS + 8, :] = latent_ref[0].astype(jnp.float32)
    for block in range(FRAMES):
        start = 6 + OWN * block
        piece = field[:, start : start + WIDE, :]
        out_ref[block] = piece.reshape(ROWS * WIDE, C).astype(jnp.bfloat16)


def pack(latent):
    return pl.pallas_call(
        pack_kernel,
        out_shape=jax.ShapeDtypeStruct((FRAMES, ROWS * WIDE, C), jnp.bfloat16),
        in_specs=[VMEM],
        out_specs=VMEM,
        scratch_shapes=[pltpu.VMEM((ROWS, COLS + 16, C), jnp.float32)],
        compiler_params=PARAMS,
    )(latent)


def conv_kernel(add, main_ref, above_ref, below_ref, gain_ref, weight_ref, *refs):
    if add:
        latent_ref, out_ref, field, stacked, total, trimmed = refs
    else:
        out_ref, field, stacked, total = refs
    gain = gain_ref[...].reshape(1, 1, C)
    field[:, :, WIDE:, :] = jnp.zeros((FRAMES, ROWS + 2, 8, C), jnp.float32)

    def act(value):
        return silu(norm_gain(value.astype(jnp.float32), gain))

    def fill(t, _):
        field[t, 0:1, 0:WIDE, :] = act(above_ref[pl.ds(t, 1)])
        field[t, ROWS + 1 :, 0:WIDE, :] = act(below_ref[pl.ds(t, 1)])
        main = main_ref[pl.ds(t, 1)].astype(jnp.float32).reshape(ROWS, WIDE, C)
        field[t, 1 : ROWS + 1, 0:WIDE, :] = act(main)
        start = pl.multiple_of(t * (ROWS * WIDE), ROWS * WIDE)
        for dh in range(3):
            for dw in range(3):
                piece = field[t, dh : dh + ROWS, dw : dw + WIDE, :]
                lanes = (dh * 3 + dw) * C
                stacked[pl.ds(start, ROWS * WIDE), lanes : lanes + C] = piece.reshape(
                    ROWS * WIDE, C
                ).astype(jnp.bfloat16)
        return 0

    lax.fori_loop(0, FRAMES, fill, 0)
    count = ROWS * WIDE
    total[...] = jnp.dot(stacked[...], weight_ref[2], preferred_element_type=jnp.float32)
    total[count:, :] += jnp.dot(
        stacked[: 7 * count, :], weight_ref[1], preferred_element_type=jnp.float32
    )
    total[2 * count :, :] += jnp.dot(
        stacked[: 6 * count, :], weight_ref[0], preferred_element_type=jnp.float32
    )
    if not add:
        out_ref[...] = total[...].astype(jnp.bfloat16).reshape(FRAMES, count, C)
        return

    def finish(t, _):
        start = pl.multiple_of(t * count, count)
        value = total[pl.ds(start, count), :].reshape(ROWS, WIDE, C)
        field[t, 0:ROWS, 8 : WIDE + 8, :] = (
            latent_ref[pl.ds(t, 1)].astype(jnp.float32).reshape(ROWS, WIDE, C)
        )
        value = value[:, :OWN, :] + field[t, 0:ROWS, 10 : OWN + 10, :]
        for row in range(ROWS):
            trimmed[row * OWN : row * OWN + OWN, :] = value[row]
        out_ref[pl.ds(t, 1)] = trimmed[...].astype(jnp.bfloat16).reshape(1, POS, C)
        return 0

    lax.fori_loop(0, FRAMES, finish, 0)


def convolve(main, above, below, gain, weight, latent=None):
    add = latent is not None
    operands = [main, above, below, gain.reshape(1, C), weight.reshape(3, 9 * C, C)]
    scratch = [
        pltpu.VMEM((FRAMES, ROWS + 2, WIDE + 8, C), jnp.float32),
        pltpu.VMEM((FRAMES * ROWS * WIDE, 9 * C), jnp.bfloat16),
        pltpu.VMEM((FRAMES * ROWS * WIDE, C), jnp.float32),
    ]
    if add:
        operands.append(latent)
        scratch.append(pltpu.VMEM((POS, C), jnp.float32))
    return pl.pallas_call(
        functools.partial(conv_kernel, add),
        out_shape=jax.ShapeDtypeStruct(
            (FRAMES, POS if add else ROWS * WIDE, C), jnp.bfloat16
        ),
        in_specs=[VMEM] * len(operands),
        out_specs=VMEM,
        scratch_shapes=scratch,
        compiler_params=PARAMS,
        cost_estimate=pl.CostEstimate(
            flops=2 * 768 * 27 * C * C, bytes_accessed=27 * C * C * 2, transcendentals=10**6
        ),
    )(*operands)


def attend_kernel(count, tile, group, first, query_ref, *refs):
    blocks = refs[:count]
    if first:
        acc_out, top_out, sum_out = refs[count:]
    else:
        acc_in, top_in, sum_in, acc_out, top_out, sum_out = refs[count:]

    def step(i, _):
        rows = pl.ds(pl.multiple_of(i * tile, tile), tile)
        query = query_ref[rows, :]
        top = summed = acc = None
        if not first:
            top, summed, acc = top_in[rows, :1], sum_in[rows, :1], acc_in[rows, :]
        for start in range(0, count, group):
            keys = [block[...] for block in blocks[start : start + group]]
            scores = [
                lax.dot_general(query, key, ROW_DOT, preferred_element_type=jnp.float32)
                for key in keys
            ]
            ceiling = scores[0].max(-1, keepdims=True)
            for score in scores[1:]:
                ceiling = jnp.maximum(ceiling, score.max(-1, keepdims=True))
            if top is not None:
                ceiling = jnp.maximum(ceiling, top)
            weights = [jnp.exp2(score - ceiling) for score in scores]
            new_sum = sum(weight.sum(-1, keepdims=True) for weight in weights)
            new_acc = sum(
                jnp.dot(weight.astype(jnp.bfloat16), key, preferred_element_type=jnp.float32)
                for weight, key in zip(weights, keys)
            )
            if top is not None:
                shrink = jnp.exp2(top - ceiling)
                new_sum = summed * shrink + new_sum
                new_acc = acc * shrink + new_acc
            top, summed, acc = ceiling, new_sum, new_acc
        acc_out[rows, :] = acc
        top_out[rows, :] = jnp.broadcast_to(top, (tile, 128))
        sum_out[rows, :] = jnp.broadcast_to(summed, (tile, 128))
        return 0

    lax.fori_loop(0, query_ref.shape[0] // tile, step, 0)


def attend(query, blocks, state=None, tile=640, group=2):
    rows = query.shape[0]
    keys = sum(block.shape[0] for block in blocks)
    operands = [query, *blocks, *(state or ())]
    return pl.pallas_call(
        functools.partial(attend_kernel, len(blocks), tile, group, state is None),
        out_shape=(
            jax.ShapeDtypeStruct((rows, C), jnp.float32),
            jax.ShapeDtypeStruct((rows, 128), jnp.float32),
            jax.ShapeDtypeStruct((rows, 128), jnp.float32),
        ),
        in_specs=[VMEM] * len(operands),
        out_specs=(VMEM, VMEM, VMEM),
        compiler_params=PARAMS,
        cost_estimate=pl.CostEstimate(
            flops=4 * rows * keys * C, bytes_accessed=2 * keys * C, transcendentals=rows * keys
        ),
    )(*operands)


def finish_kernel(
    acc_ref, top_ref, sum_ref, other_ref, level_ref, state_ref, value_ref, outw_ref, out_ref, field
):
    own = top_ref[:, :1] + jnp.log2(sum_ref[:, :1])
    other = level_ref[...]
    ceiling = jnp.maximum(own, other)
    own_part = jnp.exp2(own - ceiling)
    other_part = jnp.exp2(other - ceiling)
    mixed = acc_ref[...] * (own_part / sum_ref[:, :1]) + other_ref[...].astype(jnp.float32) * (
        other_part
    )
    mixed = (mixed / (own_part + other_part)).astype(jnp.bfloat16)
    attended = jnp.dot(mixed, value_ref[...], preferred_element_type=jnp.float32)
    result = jnp.dot(
        attended.astype(jnp.bfloat16), outw_ref[...], preferred_element_type=jnp.float32
    ) + state_ref[...].astype(jnp.float32)
    for block in range(FRAMES):
        for row in range(ROWS):
            start = (block * ROWS + row) * OWN
            field[row, block * OWN : block * OWN + OWN, :] = result[start : start + OWN, :]
    out_ref[0] = field[...].astype(jnp.bfloat16)


def finish(state, other, level, flat, value_weight, out_weight):
    return pl.pallas_call(
        finish_kernel,
        out_shape=jax.ShapeDtypeStruct((1, ROWS, COLS, C), jnp.bfloat16),
        in_specs=[VMEM] * 8,
        out_specs=VMEM,
        scratch_shapes=[pltpu.VMEM((ROWS, COLS, C), jnp.float32)],
        compiler_params=PARAMS,
    )(*state, other, level, flat, value_weight, out_weight)


def row_halos(field):
    count = lax.axis_size("tile")
    forward = [(i, i + 1) for i in range(count - 1)]
    backward = [(i + 1, i) for i in range(count - 1)]
    above = lax.ppermute(field[:, (ROWS - 1) * WIDE :, :], "tile", forward)
    below = lax.ppermute(field[:, :WIDE, :], "tile", backward)
    return above, below


def body(
    latent,
    norm1_gain,
    conv1_weight,
    norm2_gain,
    conv2_weight,
    attn_gain,
    query_weight,
    key_weight,
    value_weight,
    out_weight,
):
    field = lax.all_to_all(pack(latent), "frame", 0, 0)
    conv_one = convolve(field, *row_halos(field), norm1_gain, conv1_weight)
    column = lax.broadcasted_iota(jnp.int32, (1, ROWS, WIDE, 1), 2).reshape(1, ROWS * WIDE, 1)
    column = column + (OWN * lax.axis_index("frame") - 1)
    conv_one = jnp.where((column >= 0) & (column < COLS), conv_one, jnp.bfloat16(0))
    hstate = convolve(conv_one, *row_halos(conv_one), norm2_gain, conv2_weight, field)
    flat = lax.all_to_all(hstate, "frame", 0, 0).reshape(FRAMES * POS, C)
    normed = norm_gain(flat.astype(jnp.float32), attn_gain).astype(jnp.bfloat16)

    scale = math.log2(math.e) / math.sqrt(C)

    def query_rows(rows):
        query = jnp.dot(rows, query_weight, preferred_element_type=jnp.float32)
        query = lax.dot_general(
            query.astype(jnp.bfloat16), key_weight, ROW_DOT, preferred_element_type=jnp.float32
        )
        return (query * scale).astype(jnp.bfloat16)

    behind = send(normed, UP_X)
    ahead = send(normed, DOWN_X)
    across = send(normed, OTHER_Z)
    mate = send(normed, CORE)
    query = query_rows(normed)
    state = attend(query, [normed, mate])
    half = normed.shape[0] // 2
    far = jnp.concatenate([send(behind[:half], UP_X), send(ahead[half:], DOWN_X)], 0)
    behind_mate = send(behind, CORE)
    ahead_mate = send(ahead, CORE)
    near = [behind, ahead, behind_mate, ahead_mate]
    other_query = query_rows(across)
    other_state = attend(other_query, [normed, mate] + near)
    far_mate = send(far, CORE)
    acc, top, summed = attend(other_query, [far, far_mate], other_state)
    sent = (acc / summed[:, :1]).astype(jnp.bfloat16)
    level = (top[:, :1] + jnp.log2(summed[:, :1])).reshape(-1)
    other = send(sent, OTHER_Z)
    other_level = send(level, OTHER_Z)
    state = attend(query, near + [far, far_mate], state)
    return finish(state, other, other_level.reshape(-1, 1), flat, value_weight, out_weight)


def solution(mesh):
    return jax.shard_map(
        body,
        mesh=mesh,
        in_specs=(P("frame", "tile", None, None), P(), P(), P(), P(), P(), P(), P(), P(), P()),
        out_specs=P("frame", "tile", None, None),
        check_vma=False,
    )
```

```python
import functools
import math

import jax
import jax.numpy as jnp
from jax import lax
from jax.experimental import pallas as pl
from jax.experimental.pallas import tpu as pltpu
from jax.sharding import PartitionSpec as P

C = 384
FRAMES = 8
ROWS = 4
COLS = 160
OWN = COLS // FRAMES
WIDE = OWN + 4
POS = ROWS * OWN
BOTH = ("frame", "tile")
VMEM = pl.BlockSpec(memory_space=pltpu.VMEM)
PARAMS = pltpu.CompilerParams(vmem_limit_bytes=24 * 2**20)
CONV_PARAMS = pltpu.CompilerParams(vmem_limit_bytes=28 * 2**20)
ROW_DOT = (((1,), (1,)), ((), ()))


def coords(device):
    frame, tile = divmod(device, 16)
    return frame, tile // 4, tile // 2 % 2, tile % 2


def permutation(move):
    pairs = []
    for device in range(128):
        frame, x, z, core = move(*coords(device))
        pairs.append((device, frame * 16 + x % 4 * 4 + z % 2 * 2 + core % 2))
    return pairs


CORE = permutation(lambda f, x, z, c: (f, x, z, c + 1))
UP_X = permutation(lambda f, x, z, c: (f, x + 1, z, c))
DOWN_X = permutation(lambda f, x, z, c: (f, x - 1, z, c))
OTHER_Z = permutation(lambda f, x, z, c: (f, x, z + 1, c))


def send(value, pairs):
    return lax.ppermute(value, BOTH, pairs)


def norm_gain(field, gain):
    squares = jnp.mean(field * field, axis=-1, keepdims=True)
    return field * lax.rsqrt(squares + 1e-06) * gain.astype(jnp.float32)


def silu(u):
    return u / (1.0 + jnp.exp(-u))


def pack_kernel(latent_ref, out_ref, field):
    field[:, 0:8, :] = jnp.zeros((ROWS, 8, C), jnp.float32)
    field[:, COLS + 8 : COLS + 16, :] = jnp.zeros((ROWS, 8, C), jnp.float32)
    field[:, 8 : COLS + 8, :] = latent_ref[0].astype(jnp.float32)
    for block in range(FRAMES):
        start = 6 + OWN * block
        piece = field[:, start : start + WIDE, :]
        out_ref[block] = piece.reshape(ROWS * WIDE, C).astype(jnp.bfloat16)


def pack(latent):
    return pl.pallas_call(
        pack_kernel,
        out_shape=jax.ShapeDtypeStruct((FRAMES, ROWS * WIDE, C), jnp.bfloat16),
        in_specs=[VMEM],
        out_specs=VMEM,
        scratch_shapes=[pltpu.VMEM((ROWS, COLS + 16, C), jnp.float32)],
        compiler_params=PARAMS,
    )(latent)


COUNT = ROWS * WIDE


def activate(value, gain_ref):
    return silu(norm_gain(value, gain_ref[...].reshape(1, 1, C)))


def own_rows_kernel(main_ref, gain_ref, weight_ref, total_ref, field, stacked):
    field[:, :, WIDE:, :] = jnp.zeros((FRAMES, ROWS + 2, 8, C), jnp.float32)
    field[:, 0:1, 0:WIDE, :] = jnp.zeros((FRAMES, 1, WIDE, C), jnp.float32)
    field[:, ROWS + 1 :, 0:WIDE, :] = jnp.zeros((FRAMES, 1, WIDE, C), jnp.float32)

    def fill(t, _):
        main = main_ref[pl.ds(t, 1)].astype(jnp.float32).reshape(ROWS, WIDE, C)
        field[t, 1 : ROWS + 1, 0:WIDE, :] = activate(main, gain_ref)
        start = pl.multiple_of(t * COUNT, COUNT)
        for dh in range(3):
            for dw in range(3):
                piece = field[t, dh : dh + ROWS, dw : dw + WIDE, :]
                lanes = (dh * 3 + dw) * C
                stacked[pl.ds(start, COUNT), lanes : lanes + C] = piece.reshape(COUNT, C).astype(
                    jnp.bfloat16
                )
        return 0

    lax.fori_loop(0, FRAMES, fill, 0)
    pair = jnp.concatenate([weight_ref[2], weight_ref[1]], 1)
    both = jnp.dot(stacked[...], pair, preferred_element_type=jnp.float32)
    total_ref[...] = both[:, :C]
    total_ref[COUNT:, :] += both[: 7 * COUNT, C:]
    total_ref[2 * COUNT :, :] += jnp.dot(
        stacked[: 6 * COUNT, :], weight_ref[0], preferred_element_type=jnp.float32
    )


def edge_rows_kernel(add, total_ref, above_ref, below_ref, gain_ref, weight_ref, *refs):
    if add:
        latent_ref, out_ref, field, stacked, edge, shifted, trimmed = refs
    else:
        out_ref, field, stacked, edge = refs
    for side, rows_ref in enumerate((above_ref, below_ref)):
        field[side, :, WIDE:, :] = jnp.zeros((FRAMES, 8, C), jnp.float32)
        field[side, :, 0:WIDE, :] = activate(rows_ref[...].astype(jnp.float32), gain_ref)
        for dw in range(3):
            piece = field[side, :, dw : dw + WIDE, :]
            stacked[side, :, dw * C : dw * C + C] = piece.reshape(FRAMES * WIDE, C).astype(
                jnp.bfloat16
            )
        taps = slice(side * 6 * C, side * 6 * C + 3 * C)
        weights = jnp.concatenate([weight_ref[dt, taps, :] for dt in (2, 1, 0)], 1)
        three = jnp.dot(stacked[side], weights, preferred_element_type=jnp.float32)
        edge[side] = three[:, :C]
        edge[side, WIDE:, :] += three[: 7 * WIDE, C : 2 * C]
        edge[side, 2 * WIDE :, :] += three[: 6 * WIDE, 2 * C :]
    for t in range(FRAMES):
        value = total_ref[t * COUNT : t * COUNT + COUNT, :]
        rows = slice(t * WIDE, t * WIDE + WIDE)
        value = jnp.concatenate(
            [
                value[:WIDE] + edge[0, rows, :],
                value[WIDE : 3 * WIDE],
                value[3 * WIDE :] + edge[1, rows, :],
            ],
            0,
        )
        if not add:
            out_ref[t] = value.astype(jnp.bfloat16)
            continue
        shifted[:, 8 : WIDE + 8, :] = latent_ref[t].astype(jnp.float32).reshape(ROWS, WIDE, C)
        value = value.reshape(ROWS, WIDE, C)[:, :OWN, :] + shifted[:, 10 : OWN + 10, :]
        for row in range(ROWS):
            trimmed[row * OWN : row * OWN + OWN, :] = value[row]
        out_ref[t] = trimmed[...].astype(jnp.bfloat16)


def convolve(main, gain, weight, latent=None):
    add = latent is not None
    gain, weight = gain.reshape(1, C), weight.reshape(3, 9 * C, C)
    above, below = row_halos(main)
    total = pl.pallas_call(
        own_rows_kernel,
        out_shape=jax.ShapeDtypeStruct((FRAMES * COUNT, C), jnp.float32),
        in_specs=[VMEM] * 3,
        out_specs=VMEM,
        scratch_shapes=[
            pltpu.VMEM((FRAMES, ROWS + 2, WIDE + 8, C), jnp.float32),
            pltpu.VMEM((FRAMES * COUNT, 9 * C), jnp.bfloat16),
        ],
        compiler_params=CONV_PARAMS,
        cost_estimate=pl.CostEstimate(
            flops=2 * 768 * 27 * C * C, bytes_accessed=27 * C * C * 2, transcendentals=10**6
        ),
    )(main, gain, weight)
    operands = [total, above, below, gain, weight]
    scratch = [
        pltpu.VMEM((2, FRAMES, WIDE + 8, C), jnp.float32),
        pltpu.VMEM((2, FRAMES * WIDE, 3 * C), jnp.bfloat16),
        pltpu.VMEM((2, FRAMES * WIDE, C), jnp.float32),
    ]
    if add:
        operands.append(latent)
        scratch.append(pltpu.VMEM((ROWS, WIDE + 8, C), jnp.float32))
        scratch.append(pltpu.VMEM((POS, C), jnp.float32))
    return pl.pallas_call(
        functools.partial(edge_rows_kernel, add),
        out_shape=jax.ShapeDtypeStruct((FRAMES, POS if add else COUNT, C), jnp.bfloat16),
        in_specs=[VMEM] * len(operands),
        out_specs=VMEM,
        scratch_shapes=scratch,
        compiler_params=CONV_PARAMS,
        cost_estimate=pl.CostEstimate(
            flops=2 * 384 * 9 * C * C, bytes_accessed=27 * C * C * 2, transcendentals=10**5
        ),
    )(*operands)


def attend_kernel(count, group, start, end, *refs):
    if start:
        rows_ref, query_weight_ref, key_weight_ref = refs[:3]
        refs = refs[3:]
        scale = math.log2(math.e) / math.sqrt(C)
        query = jnp.dot(
            rows_ref[...], query_weight_ref[...], preferred_element_type=jnp.float32
        ).astype(jnp.bfloat16)
        query = lax.dot_general(
            query, key_weight_ref[...], ROW_DOT, preferred_element_type=jnp.float32
        )
        query = (query * scale).astype(jnp.bfloat16)
        top = summed = acc = None
    else:
        query_ref, acc_in, top_in, sum_in = refs[:4]
        refs = refs[4:]
        query = query_ref[...]
        top, summed, acc = top_in[:, :1], sum_in[:, :1], acc_in[...]
    blocks, outs = refs[:count], refs[count:]
    for first in range(0, count, group):
        keys = [block[...] for block in blocks[first : first + group]]
        scores = [
            lax.dot_general(query, key, ROW_DOT, preferred_element_type=jnp.float32)
            for key in keys
        ]
        ceiling = scores[0].max(-1, keepdims=True)
        for score in scores[1:]:
            ceiling = jnp.maximum(ceiling, score.max(-1, keepdims=True))
        if top is not None:
            ceiling = jnp.maximum(ceiling, top)
        weights = [jnp.exp2(score - ceiling) for score in scores]
        new_sum = sum(weight.sum(-1, keepdims=True) for weight in weights)
        new_acc = sum(
            jnp.dot(weight.astype(jnp.bfloat16), key, preferred_element_type=jnp.float32)
            for weight, key in zip(weights, keys)
        )
        if top is not None:
            shrink = jnp.exp2(top - ceiling)
            new_sum = summed * shrink + new_sum
            new_acc = acc * shrink + new_acc
        top, summed, acc = ceiling, new_sum, new_acc
    if end:
        share_out, level_out = outs
        share_out[...] = (acc / summed).astype(jnp.bfloat16)
        level_out[...] = jnp.broadcast_to(top + jnp.log2(summed), level_out.shape)
        return
    if start:
        outs[0][...] = query
        outs = outs[1:]
    acc_out, top_out, sum_out = outs
    acc_out[...] = acc
    top_out[...] = jnp.broadcast_to(top, top_out.shape)
    sum_out[...] = jnp.broadcast_to(summed, sum_out.shape)


def attend(source, blocks, group=2, start=False, end=False):
    rows = source[0].shape[0]
    keys = sum(block.shape[0] for block in blocks)
    operands = [*source, *blocks]
    bf16 = jax.ShapeDtypeStruct((rows, C), jnp.bfloat16)
    column = jax.ShapeDtypeStruct((rows, 128), jnp.float32)
    outs = (jax.ShapeDtypeStruct((rows, C), jnp.float32), column, column)
    if end:
        outs = (bf16, column)
    elif start:
        outs = (bf16, *outs)
    return pl.pallas_call(
        functools.partial(attend_kernel, len(blocks), group, start, end),
        out_shape=outs,
        in_specs=[VMEM] * len(operands),
        out_specs=tuple(VMEM for _ in outs),
        compiler_params=PARAMS,
        cost_estimate=pl.CostEstimate(
            flops=4 * rows * keys * C, bytes_accessed=2 * keys * C, transcendentals=rows * keys
        ),
    )(*operands)


def finish_kernel(
    acc_ref, top_ref, sum_ref, other_ref, level_ref, state_ref, value_ref, outw_ref, out_ref, field
):
    own = top_ref[:, :1] + jnp.log2(sum_ref[:, :1])
    other = level_ref[...]
    ceiling = jnp.maximum(own, other)
    own_part = jnp.exp2(own - ceiling)
    other_part = jnp.exp2(other - ceiling)
    mixed = acc_ref[...] * (own_part / sum_ref[:, :1]) + other_ref[...].astype(jnp.float32) * (
        other_part
    )
    mixed = (mixed / (own_part + other_part)).astype(jnp.bfloat16)
    attended = jnp.dot(mixed, value_ref[...], preferred_element_type=jnp.float32)
    result = jnp.dot(
        attended.astype(jnp.bfloat16), outw_ref[...], preferred_element_type=jnp.float32
    ) + state_ref[...].astype(jnp.float32)
    for block in range(FRAMES):
        for row in range(ROWS):
            start = (block * ROWS + row) * OWN
            field[row, block * OWN : block * OWN + OWN, :] = result[start : start + OWN, :]
    out_ref[0] = field[...].astype(jnp.bfloat16)


def finish(state, other, level, flat, value_weight, out_weight):
    return pl.pallas_call(
        finish_kernel,
        out_shape=jax.ShapeDtypeStruct((1, ROWS, COLS, C), jnp.bfloat16),
        in_specs=[VMEM] * 8,
        out_specs=VMEM,
        scratch_shapes=[pltpu.VMEM((ROWS, COLS, C), jnp.float32)],
        compiler_params=PARAMS,
    )(*state, other, level, flat, value_weight, out_weight)


def row_halos(field):
    count = lax.axis_size("tile")
    forward = [(i, i + 1) for i in range(count - 1)]
    backward = [(i + 1, i) for i in range(count - 1)]
    above = lax.ppermute(field[:, (ROWS - 1) * WIDE :, :], "tile", forward)
    below = lax.ppermute(field[:, :WIDE, :], "tile", backward)
    return above, below


def body(
    latent,
    norm1_gain,
    conv1_weight,
    norm2_gain,
    conv2_weight,
    attn_gain,
    query_weight,
    key_weight,
    value_weight,
    out_weight,
):
    field = lax.all_to_all(pack(latent), "frame", 0, 0)
    conv_one = convolve(field, norm1_gain, conv1_weight)
    column = lax.broadcasted_iota(jnp.int32, (1, ROWS, WIDE, 1), 2).reshape(1, COUNT, 1)
    column = column + (OWN * lax.axis_index("frame") - 1)
    conv_one = jnp.where((column >= 0) & (column < COLS), conv_one, jnp.bfloat16(0))
    hstate = convolve(conv_one, norm2_gain, conv2_weight, field)
    flat = lax.all_to_all(hstate, "frame", 0, 0).reshape(FRAMES * POS, C)
    normed = norm_gain(flat.astype(jnp.float32), attn_gain).astype(jnp.bfloat16)
    half = normed.shape[0] // 2
    low, high = normed[:half], normed[half:]
    behind_low = send(low, UP_X)
    ahead_high = send(high, DOWN_X)
    mate = send(normed, CORE)
    behind_high = send(high, UP_X)
    ahead_low = send(low, DOWN_X)
    across = send(normed, OTHER_Z)
    own = attend([normed, query_weight, key_weight], [normed, mate], start=True)
    (behind_low, ahead_high, own) = lax.optimization_barrier((behind_low, ahead_high, own))
    far_low = send(behind_low, UP_X)
    far_high = send(ahead_high, DOWN_X)
    early = jnp.concatenate([behind_low, ahead_high], 0)
    early_mate = send(early, CORE)
    late = jnp.concatenate([behind_high, ahead_low], 0)
    late_mate = send(late, CORE)
    other = attend([across, query_weight, key_weight], [normed, mate, early, late], start=True)
    far = jnp.concatenate([far_low, far_high], 0)
    far_mate = send(far, CORE)
    other_query = other[0]
    other = attend(other, [early_mate, late_mate])
    share, level = attend([other_query, *other], [far, far_mate], end=True)
    share_back = send(share, OTHER_Z)
    level_back = send(level[:, 0], OTHER_Z)
    own = lax.optimization_barrier((own, share))[0]
    own = attend(own, [early, late, early_mate, late_mate, far, far_mate])
    return finish(own, share_back, level_back.reshape(-1, 1), flat, value_weight, out_weight)


def solution(mesh):
    return jax.shard_map(
        body,
        mesh=mesh,
        in_specs=(P("frame", "tile", None, None), P(), P(), P(), P(), P(), P(), P(), P(), P()),
        out_specs=P("frame", "tile", None, None),
        check_vma=False,
    )
```

```python
import functools
import math

import jax
import jax.numpy as jnp
from jax import lax
from jax.experimental import pallas as pl
from jax.experimental.pallas import tpu as pltpu
from jax.sharding import PartitionSpec as P

C = 384
FRAMES = 8
ROWS = 4
COLS = 160
OWN = COLS // FRAMES
WIDE = OWN + 4
POS = ROWS * OWN
BOTH = ("frame", "tile")
VMEM = pl.BlockSpec(memory_space=pltpu.VMEM)
PARAMS = pltpu.CompilerParams(vmem_limit_bytes=24 * 2**20)
CONV_PARAMS = pltpu.CompilerParams(vmem_limit_bytes=34 * 2**20)
ROW_DOT = (((1,), (1,)), ((), ()))


def coords(device):
    frame, tile = divmod(device, 16)
    return frame, tile // 4, tile // 2 % 2, tile % 2


def permutation(move):
    pairs = []
    for device in range(128):
        frame, x, z, core = move(*coords(device))
        pairs.append((device, frame * 16 + x % 4 * 4 + z % 2 * 2 + core % 2))
    return pairs


CORE = permutation(lambda f, x, z, c: (f, x, z, c + 1))
UP_X = permutation(lambda f, x, z, c: (f, x + 1, z, c))
DOWN_X = permutation(lambda f, x, z, c: (f, x - 1, z, c))
OTHER_Z = permutation(lambda f, x, z, c: (f, x, z + 1, c))


def send(value, pairs):
    return lax.ppermute(value, BOTH, pairs)


def norm_gain(field, gain):
    squares = jnp.mean(field * field, axis=-1, keepdims=True)
    return field * lax.rsqrt(squares + 1e-06) * gain.astype(jnp.float32)


def silu(u):
    return u / (1.0 + jnp.exp(-u))


def pack_kernel(latent_ref, out_ref, field):
    field[:, 0:8, :] = jnp.zeros((ROWS, 8, C), jnp.float32)
    field[:, COLS + 8 : COLS + 16, :] = jnp.zeros((ROWS, 8, C), jnp.float32)
    field[:, 8 : COLS + 8, :] = latent_ref[0].astype(jnp.float32)
    for block in range(FRAMES):
        start = 6 + OWN * block
        piece = field[:, start : start + WIDE, :]
        out_ref[block] = piece.reshape(ROWS * WIDE, C).astype(jnp.bfloat16)


def pack(latent):
    return pl.pallas_call(
        pack_kernel,
        out_shape=jax.ShapeDtypeStruct((FRAMES, ROWS * WIDE, C), jnp.bfloat16),
        in_specs=[VMEM],
        out_specs=VMEM,
        scratch_shapes=[pltpu.VMEM((ROWS, COLS + 16, C), jnp.float32)],
        compiler_params=PARAMS,
    )(latent)


COUNT = ROWS * WIDE


def activate(value, gain_ref):
    return silu(norm_gain(value, gain_ref[...].reshape(1, 1, C)))


def own_rows_kernel(main_ref, gain_ref, weight_hbm, total_ref, field, stacked, weight_ref, arrived):
    copies = [
        pltpu.make_async_copy(weight_hbm.at[dt], weight_ref.at[dt], arrived.at[dt])
        for dt in range(3)
    ]
    for dt in (2, 1, 0):
        copies[dt].start()
    field[:, :, WIDE:, :] = jnp.zeros((FRAMES, ROWS + 2, 8, C), jnp.float32)
    field[:, 0:1, 0:WIDE, :] = jnp.zeros((FRAMES, 1, WIDE, C), jnp.float32)
    field[:, ROWS + 1 :, 0:WIDE, :] = jnp.zeros((FRAMES, 1, WIDE, C), jnp.float32)

    def fill(t, _):
        main = main_ref[pl.ds(t, 1)].astype(jnp.float32).reshape(ROWS, WIDE, C)
        field[t, 1 : ROWS + 1, 0:WIDE, :] = activate(main, gain_ref)
        start = pl.multiple_of(t * COUNT, COUNT)
        for dh in range(3):
            for dw in range(3):
                piece = field[t, dh : dh + ROWS, dw : dw + WIDE, :]
                lanes = (dh * 3 + dw) * C
                stacked[pl.ds(start, COUNT), lanes : lanes + C] = piece.reshape(COUNT, C).astype(
                    jnp.bfloat16
                )
        return 0

    lax.fori_loop(0, FRAMES, fill, 0)
    copies[2].wait()
    copies[1].wait()
    pair = jnp.concatenate([weight_ref[2], weight_ref[1]], 1)
    both = jnp.dot(stacked[...], pair, preferred_element_type=jnp.float32)
    total_ref[...] = both[:, :C]
    total_ref[COUNT:, :] += both[: 7 * COUNT, C:]
    copies[0].wait()
    total_ref[2 * COUNT :, :] += jnp.dot(
        stacked[: 6 * COUNT, :], weight_ref[0], preferred_element_type=jnp.float32
    )


def edge_rows_kernel(add, total_ref, above_ref, below_ref, gain_ref, weight_ref, *refs):
    if add:
        latent_ref, out_ref, field, stacked, edge, shifted, trimmed = refs
    else:
        out_ref, field, stacked, edge = refs
    for side, rows_ref in enumerate((above_ref, below_ref)):
        field[side, :, WIDE:, :] = jnp.zeros((FRAMES, 8, C), jnp.float32)
        field[side, :, 0:WIDE, :] = activate(rows_ref[...].astype(jnp.float32), gain_ref)
        for dw in range(3):
            piece = field[side, :, dw : dw + WIDE, :]
            stacked[side, :, dw * C : dw * C + C] = piece.reshape(FRAMES * WIDE, C).astype(
                jnp.bfloat16
            )
        taps = slice(side * 6 * C, side * 6 * C + 3 * C)
        weights = jnp.concatenate([weight_ref[dt, taps, :] for dt in (2, 1, 0)], 1)
        three = jnp.dot(stacked[side], weights, preferred_element_type=jnp.float32)
        edge[side] = three[:, :C]
        edge[side, WIDE:, :] += three[: 7 * WIDE, C : 2 * C]
        edge[side, 2 * WIDE :, :] += three[: 6 * WIDE, 2 * C :]
    for t in range(FRAMES):
        value = total_ref[t * COUNT : t * COUNT + COUNT, :]
        rows = slice(t * WIDE, t * WIDE + WIDE)
        value = jnp.concatenate(
            [
                value[:WIDE] + edge[0, rows, :],
                value[WIDE : 3 * WIDE],
                value[3 * WIDE :] + edge[1, rows, :],
            ],
            0,
        )
        if not add:
            out_ref[t] = value.astype(jnp.bfloat16)
            continue
        shifted[:, 8 : WIDE + 8, :] = latent_ref[t].astype(jnp.float32).reshape(ROWS, WIDE, C)
        value = value.reshape(ROWS, WIDE, C)[:, :OWN, :] + shifted[:, 10 : OWN + 10, :]
        for row in range(ROWS):
            trimmed[row * OWN : row * OWN + OWN, :] = value[row]
        out_ref[t] = trimmed[...].astype(jnp.bfloat16)


def convolve(main, gain, weight, latent=None):
    add = latent is not None
    gain, weight = gain.reshape(1, C), weight.reshape(3, 9 * C, C)
    above, below = row_halos(main)
    total = pl.pallas_call(
        own_rows_kernel,
        out_shape=jax.ShapeDtypeStruct((FRAMES * COUNT, C), jnp.float32),
        in_specs=[VMEM, VMEM, pl.BlockSpec(memory_space=pltpu.HBM)],
        out_specs=VMEM,
        scratch_shapes=[
            pltpu.VMEM((FRAMES, ROWS + 2, WIDE + 8, C), jnp.float32),
            pltpu.VMEM((FRAMES * COUNT, 9 * C), jnp.bfloat16),
            pltpu.VMEM((3, 9 * C, C), jnp.bfloat16),
            pltpu.SemaphoreType.DMA((3,)),
        ],
        compiler_params=CONV_PARAMS,
        cost_estimate=pl.CostEstimate(
            flops=2 * 768 * 27 * C * C, bytes_accessed=27 * C * C * 2, transcendentals=10**6
        ),
    )(main, gain, pltpu.with_memory_space_constraint(weight, pltpu.HBM))
    operands = [total, above, below, gain, weight]
    scratch = [
        pltpu.VMEM((2, FRAMES, WIDE + 8, C), jnp.float32),
        pltpu.VMEM((2, FRAMES * WIDE, 3 * C), jnp.bfloat16),
        pltpu.VMEM((2, FRAMES * WIDE, C), jnp.float32),
    ]
    if add:
        operands.append(latent)
        scratch.append(pltpu.VMEM((ROWS, WIDE + 8, C), jnp.float32))
        scratch.append(pltpu.VMEM((POS, C), jnp.float32))
    return pl.pallas_call(
        functools.partial(edge_rows_kernel, add),
        out_shape=jax.ShapeDtypeStruct((FRAMES, POS if add else COUNT, C), jnp.bfloat16),
        in_specs=[VMEM] * len(operands),
        out_specs=VMEM,
        scratch_shapes=scratch,
        compiler_params=CONV_PARAMS,
        cost_estimate=pl.CostEstimate(
            flops=2 * 384 * 9 * C * C, bytes_accessed=27 * C * C * 2, transcendentals=10**5
        ),
    )(*operands)


def attend_kernel(count, group, start, end, *refs):
    if start:
        rows_ref, query_weight_ref, key_weight_ref = refs[:3]
        refs = refs[3:]
        scale = math.log2(math.e) / math.sqrt(C)
        query = jnp.dot(
            rows_ref[...], query_weight_ref[...], preferred_element_type=jnp.float32
        ).astype(jnp.bfloat16)
        query = lax.dot_general(
            query, key_weight_ref[...], ROW_DOT, preferred_element_type=jnp.float32
        )
        query = (query * scale).astype(jnp.bfloat16)
        top = summed = acc = None
    else:
        query_ref, acc_in, top_in, sum_in = refs[:4]
        refs = refs[4:]
        query = query_ref[...]
        top, summed, acc = top_in[:, :1], sum_in[:, :1], acc_in[...]
    blocks, outs = refs[:count], refs[count:]
    for first in range(0, count, group):
        keys = [block[...] for block in blocks[first : first + group]]
        scores = [
            lax.dot_general(query, key, ROW_DOT, preferred_element_type=jnp.float32)
            for key in keys
        ]
        ceiling = scores[0].max(-1, keepdims=True)
        for score in scores[1:]:
            ceiling = jnp.maximum(ceiling, score.max(-1, keepdims=True))
        if top is not None:
            ceiling = jnp.maximum(ceiling, top)
        weights = [jnp.exp2(score - ceiling) for score in scores]
        new_sum = sum(weight.sum(-1, keepdims=True) for weight in weights)
        new_acc = sum(
            jnp.dot(weight.astype(jnp.bfloat16), key, preferred_element_type=jnp.float32)
            for weight, key in zip(weights, keys)
        )
        if top is not None:
            shrink = jnp.exp2(top - ceiling)
            new_sum = summed * shrink + new_sum
            new_acc = acc * shrink + new_acc
        top, summed, acc = ceiling, new_sum, new_acc
    if end:
        share_out, level_out = outs
        share_out[...] = (acc / summed).astype(jnp.bfloat16)
        level_out[...] = jnp.broadcast_to(top + jnp.log2(summed), level_out.shape)
        return
    if start:
        outs[0][...] = query
        outs = outs[1:]
    acc_out, top_out, sum_out = outs
    acc_out[...] = acc
    top_out[...] = jnp.broadcast_to(top, top_out.shape)
    sum_out[...] = jnp.broadcast_to(summed, sum_out.shape)


def attend(source, blocks, group=2, start=False, end=False):
    rows = source[0].shape[0]
    keys = sum(block.shape[0] for block in blocks)
    operands = [*source, *blocks]
    bf16 = jax.ShapeDtypeStruct((rows, C), jnp.bfloat16)
    column = jax.ShapeDtypeStruct((rows, 128), jnp.float32)
    outs = (jax.ShapeDtypeStruct((rows, C), jnp.float32), column, column)
    if end:
        outs = (bf16, column)
    elif start:
        outs = (bf16, *outs)
    return pl.pallas_call(
        functools.partial(attend_kernel, len(blocks), group, start, end),
        out_shape=outs,
        in_specs=[VMEM] * len(operands),
        out_specs=tuple(VMEM for _ in outs),
        compiler_params=PARAMS,
        cost_estimate=pl.CostEstimate(
            flops=4 * rows * keys * C, bytes_accessed=2 * keys * C, transcendentals=rows * keys
        ),
    )(*operands)


def finish_kernel(
    acc_ref, top_ref, sum_ref, other_ref, level_ref, state_ref, value_ref, outw_ref, out_ref, field
):
    own = top_ref[:, :1] + jnp.log2(sum_ref[:, :1])
    other = level_ref[...]
    ceiling = jnp.maximum(own, other)
    own_part = jnp.exp2(own - ceiling)
    other_part = jnp.exp2(other - ceiling)
    mixed = acc_ref[...] * (own_part / sum_ref[:, :1]) + other_ref[...].astype(jnp.float32) * (
        other_part
    )
    mixed = (mixed / (own_part + other_part)).astype(jnp.bfloat16)
    attended = jnp.dot(mixed, value_ref[...], preferred_element_type=jnp.float32)
    result = jnp.dot(
        attended.astype(jnp.bfloat16), outw_ref[...], preferred_element_type=jnp.float32
    ) + state_ref[...].astype(jnp.float32)
    for block in range(FRAMES):
        for row in range(ROWS):
            start = (block * ROWS + row) * OWN
            field[row, block * OWN : block * OWN + OWN, :] = result[start : start + OWN, :]
    out_ref[0] = field[...].astype(jnp.bfloat16)


def finish(state, other, level, flat, value_weight, out_weight):
    return pl.pallas_call(
        finish_kernel,
        out_shape=jax.ShapeDtypeStruct((1, ROWS, COLS, C), jnp.bfloat16),
        in_specs=[VMEM] * 8,
        out_specs=VMEM,
        scratch_shapes=[pltpu.VMEM((ROWS, COLS, C), jnp.float32)],
        compiler_params=PARAMS,
    )(*state, other, level, flat, value_weight, out_weight)


def row_halos(field):
    count = lax.axis_size("tile")
    forward = [(i, i + 1) for i in range(count - 1)]
    backward = [(i + 1, i) for i in range(count - 1)]
    above = lax.ppermute(field[:, (ROWS - 1) * WIDE :, :], "tile", forward)
    below = lax.ppermute(field[:, :WIDE, :], "tile", backward)
    return above, below


def body(
    latent,
    norm1_gain,
    conv1_weight,
    norm2_gain,
    conv2_weight,
    attn_gain,
    query_weight,
    key_weight,
    value_weight,
    out_weight,
):
    field = lax.all_to_all(pack(latent), "frame", 0, 0)
    conv_one = convolve(field, norm1_gain, conv1_weight)
    column = lax.broadcasted_iota(jnp.int32, (1, ROWS, WIDE, 1), 2).reshape(1, COUNT, 1)
    column = column + (OWN * lax.axis_index("frame") - 1)
    conv_one = jnp.where((column >= 0) & (column < COLS), conv_one, jnp.bfloat16(0))
    hstate = convolve(conv_one, norm2_gain, conv2_weight, field)
    flat = lax.all_to_all(hstate, "frame", 0, 0).reshape(FRAMES * POS, C)
    normed = norm_gain(flat.astype(jnp.float32), attn_gain).astype(jnp.bfloat16)
    half = normed.shape[0] // 2
    low, high = normed[:half], normed[half:]
    behind_low = send(low, UP_X)
    ahead_high = send(high, DOWN_X)
    across = send(normed, OTHER_Z)
    mate = send(normed, CORE)
    normed, mate, low, high = lax.optimization_barrier((normed, mate, low, high))
    behind_high = send(high, UP_X)
    ahead_low = send(low, DOWN_X)
    own = attend([normed, query_weight, key_weight], [normed, mate], start=True)
    (behind_low, ahead_high, own) = lax.optimization_barrier((behind_low, ahead_high, own))
    far_low = send(behind_low, UP_X)
    far_high = send(ahead_high, DOWN_X)
    early = jnp.concatenate([behind_low, ahead_high], 0)
    early_mate = send(early, CORE)
    late = jnp.concatenate([behind_high, ahead_low], 0)
    late_mate = send(late, CORE)
    other = attend([across, query_weight, key_weight], [normed, mate, early, late], start=True)
    (far_low, far_high, other) = lax.optimization_barrier((far_low, far_high, other))
    far = jnp.concatenate([far_low, far_high], 0)
    far_mate = send(far, CORE)
    other_query = other[0]
    other = attend(other, [early_mate, late_mate])
    share, level = attend([other_query, *other], [far, far_mate], end=True)
    share_back = send(share, OTHER_Z)
    level_back = send(level[:, 0], OTHER_Z)
    own = lax.optimization_barrier((own, share))[0]
    own = attend(own, [early, late, early_mate, late_mate, far, far_mate])
    return finish(own, share_back, level_back.reshape(-1, 1), flat, value_weight, out_weight)


def solution(mesh):
    return jax.shard_map(
        body,
        mesh=mesh,
        in_specs=(P("frame", "tile", None, None), P(), P(), P(), P(), P(), P(), P(), P(), P()),
        out_specs=P("frame", "tile", None, None),
        check_vma=False,
    )
```

```python
import functools
import math

import jax
import jax.numpy as jnp
from jax import lax
from jax.experimental import pallas as pl
from jax.experimental.pallas import tpu as pltpu
from jax.sharding import PartitionSpec as P

C = 384
FRAMES = 8
ROWS = 4
COLS = 160
OWN = COLS // FRAMES
WIDE = OWN + 4
POS = ROWS * OWN
BOTH = ("frame", "tile")
VMEM = pl.BlockSpec(memory_space=pltpu.VMEM)
PARAMS = pltpu.CompilerParams(vmem_limit_bytes=24 * 2**20)
CONV_PARAMS = pltpu.CompilerParams(vmem_limit_bytes=28 * 2**20)
STREAM_PARAMS = pltpu.CompilerParams(vmem_limit_bytes=34 * 2**20)
ROW_DOT = (((1,), (1,)), ((), ()))


def coords(device):
    frame, tile = divmod(device, 16)
    return frame, tile // 4, tile // 2 % 2, tile % 2


def permutation(move):
    pairs = []
    for device in range(128):
        frame, x, z, core = move(*coords(device))
        pairs.append((device, frame * 16 + x % 4 * 4 + z % 2 * 2 + core % 2))
    return pairs


CORE = permutation(lambda f, x, z, c: (f, x, z, c + 1))
UP_X = permutation(lambda f, x, z, c: (f, x + 1, z, c))
DOWN_X = permutation(lambda f, x, z, c: (f, x - 1, z, c))
OTHER_Z = permutation(lambda f, x, z, c: (f, x, z + 1, c))

NEXT_CHIP = [
    (f * 16 + i, f * 16 + (i + (1 if i % 2 else 15)) % 16) for f in range(FRAMES) for i in range(16)
]


def send(value, pairs):
    return lax.ppermute(value, BOTH, pairs)


def norm_gain(field, gain):
    squares = jnp.mean(field * field, axis=-1, keepdims=True)
    return field * lax.rsqrt(squares + 1e-06) * gain.astype(jnp.float32)


def silu(u):
    return u / (1.0 + jnp.exp(-u))


def pack_kernel(latent_ref, out_ref, field):
    field[:, 0:8, :] = jnp.zeros((ROWS, 8, C), jnp.float32)
    field[:, COLS + 8 : COLS + 16, :] = jnp.zeros((ROWS, 8, C), jnp.float32)
    field[:, 8 : COLS + 8, :] = latent_ref[0].astype(jnp.float32)
    for block in range(FRAMES):
        start = 6 + OWN * block
        piece = field[:, start : start + WIDE, :]
        out_ref[block] = piece.reshape(ROWS * WIDE, C).astype(jnp.bfloat16)


def pack(latent):
    return pl.pallas_call(
        pack_kernel,
        out_shape=jax.ShapeDtypeStruct((FRAMES, ROWS * WIDE, C), jnp.bfloat16),
        in_specs=[VMEM],
        out_specs=VMEM,
        scratch_shapes=[pltpu.VMEM((ROWS, COLS + 16, C), jnp.float32)],
        compiler_params=PARAMS,
    )(latent)


COUNT = ROWS * WIDE


def activate(value, gain_ref):
    return silu(norm_gain(value, gain_ref[...].reshape(1, 1, C)))


def own_rows_kernel(streamed, main_ref, gain_ref, weight_ref, total_ref, field, stacked, *refs):
    if streamed:
        source, (weight_ref, arrived) = weight_ref, refs
        copies = [
            pltpu.make_async_copy(source.at[dt], weight_ref.at[dt], arrived.at[dt])
            for dt in range(3)
        ]
        for copy in copies:
            copy.start()
    field[:, :, WIDE:, :] = jnp.zeros((FRAMES, ROWS + 2, 8, C), jnp.float32)
    field[:, 0:1, 0:WIDE, :] = jnp.zeros((FRAMES, 1, WIDE, C), jnp.float32)
    field[:, ROWS + 1 :, 0:WIDE, :] = jnp.zeros((FRAMES, 1, WIDE, C), jnp.float32)

    def fill(t, _):
        main = main_ref[pl.ds(t, 1)].astype(jnp.float32).reshape(ROWS, WIDE, C)
        field[t, 1 : ROWS + 1, 0:WIDE, :] = activate(main, gain_ref)
        start = pl.multiple_of(t * COUNT, COUNT)
        for dh in range(3):
            for dw in range(3):
                piece = field[t, dh : dh + ROWS, dw : dw + WIDE, :]
                lanes = (dh * 3 + dw) * C
                stacked[pl.ds(start, COUNT), lanes : lanes + C] = piece.reshape(COUNT, C).astype(
                    jnp.bfloat16
                )
        return 0

    lax.fori_loop(0, FRAMES, fill, 0)
    if streamed:
        for copy in copies:
            copy.wait()
    pair = jnp.concatenate([weight_ref[2], weight_ref[1]], 1)
    both = jnp.dot(stacked[...], pair, preferred_element_type=jnp.float32)
    total_ref[...] = both[:, :C]
    total_ref[COUNT:, :] += both[: 7 * COUNT, C:]
    total_ref[2 * COUNT :, :] += jnp.dot(
        stacked[: 6 * COUNT, :], weight_ref[0], preferred_element_type=jnp.float32
    )


def edge_rows_kernel(add, total_ref, above_ref, below_ref, gain_ref, weight_ref, *refs):
    if add:
        latent_ref, out_ref, field, stacked, edge, shifted, trimmed = refs
    else:
        out_ref, field, stacked, edge = refs
    for side, rows_ref in enumerate((above_ref, below_ref)):
        field[side, :, WIDE:, :] = jnp.zeros((FRAMES, 8, C), jnp.float32)
        field[side, :, 0:WIDE, :] = activate(rows_ref[...].astype(jnp.float32), gain_ref)
        for dw in range(3):
            piece = field[side, :, dw : dw + WIDE, :]
            stacked[side, :, dw * C : dw * C + C] = piece.reshape(FRAMES * WIDE, C).astype(
                jnp.bfloat16
            )
        taps = slice(side * 6 * C, side * 6 * C + 3 * C)
        weights = jnp.concatenate([weight_ref[dt, taps, :] for dt in (2, 1, 0)], 1)
        three = jnp.dot(stacked[side], weights, preferred_element_type=jnp.float32)
        edge[side] = three[:, :C]
        edge[side, WIDE:, :] += three[: 7 * WIDE, C : 2 * C]
        edge[side, 2 * WIDE :, :] += three[: 6 * WIDE, 2 * C :]
    for t in range(FRAMES):
        value = total_ref[t * COUNT : t * COUNT + COUNT, :]
        rows = slice(t * WIDE, t * WIDE + WIDE)
        value = jnp.concatenate(
            [
                value[:WIDE] + edge[0, rows, :],
                value[WIDE : 3 * WIDE],
                value[3 * WIDE :] + edge[1, rows, :],
            ],
            0,
        )
        if not add:
            out_ref[t] = value.astype(jnp.bfloat16)
            continue
        shifted[:, 8 : WIDE + 8, :] = latent_ref[t].astype(jnp.float32).reshape(ROWS, WIDE, C)
        value = value.reshape(ROWS, WIDE, C)[:, :OWN, :] + shifted[:, 10 : OWN + 10, :]
        for row in range(ROWS):
            trimmed[row * OWN : row * OWN + OWN, :] = value[row]
        out_ref[t] = trimmed[...].astype(jnp.bfloat16)


def convolve(main, gain, weight, latent=None):
    add = latent is not None
    gain, weight = gain.reshape(1, C), weight.reshape(3, 9 * C, C)
    above, below = row_halos(main)
    streamed = not add
    total = pl.pallas_call(
        functools.partial(own_rows_kernel, streamed),
        out_shape=jax.ShapeDtypeStruct((FRAMES * COUNT, C), jnp.float32),
        in_specs=[VMEM, VMEM, pl.BlockSpec(memory_space=pltpu.HBM) if streamed else VMEM],
        out_specs=VMEM,
        scratch_shapes=[
            pltpu.VMEM((FRAMES, ROWS + 2, WIDE + 8, C), jnp.float32),
            pltpu.VMEM((FRAMES * COUNT, 9 * C), jnp.bfloat16),
        ]
        + streamed * [pltpu.VMEM((3, 9 * C, C), jnp.bfloat16), pltpu.SemaphoreType.DMA((3,))],
        compiler_params=STREAM_PARAMS if streamed else CONV_PARAMS,
        cost_estimate=pl.CostEstimate(
            flops=2 * 768 * 27 * C * C, bytes_accessed=27 * C * C * 2, transcendentals=10**6
        ),
    )(main, gain, pltpu.with_memory_space_constraint(weight, pltpu.HBM) if streamed else weight)
    operands = [total, above, below, gain, weight]
    scratch = [
        pltpu.VMEM((2, FRAMES, WIDE + 8, C), jnp.float32),
        pltpu.VMEM((2, FRAMES * WIDE, 3 * C), jnp.bfloat16),
        pltpu.VMEM((2, FRAMES * WIDE, C), jnp.float32),
    ]
    if add:
        operands.append(latent)
        scratch.append(pltpu.VMEM((ROWS, WIDE + 8, C), jnp.float32))
        scratch.append(pltpu.VMEM((POS, C), jnp.float32))
    return pl.pallas_call(
        functools.partial(edge_rows_kernel, add),
        out_shape=jax.ShapeDtypeStruct((FRAMES, POS if add else COUNT, C), jnp.bfloat16),
        in_specs=[VMEM] * len(operands),
        out_specs=VMEM,
        scratch_shapes=scratch,
        compiler_params=CONV_PARAMS,
        cost_estimate=pl.CostEstimate(
            flops=2 * 384 * 9 * C * C, bytes_accessed=27 * C * C * 2, transcendentals=10**5
        ),
    )(*operands)


def attend_kernel(count, group, start, end, *refs):
    if start:
        rows_ref, query_weight_ref, key_weight_ref = refs[:3]
        refs = refs[3:]
        scale = math.log2(math.e) / math.sqrt(C)
        query = jnp.dot(
            rows_ref[...], query_weight_ref[...], preferred_element_type=jnp.float32
        ).astype(jnp.bfloat16)
        query = lax.dot_general(
            query, key_weight_ref[...], ROW_DOT, preferred_element_type=jnp.float32
        )
        query = (query * scale).astype(jnp.bfloat16)
        top = summed = acc = None
    else:
        query_ref, acc_in, top_in, sum_in = refs[:4]
        refs = refs[4:]
        query = query_ref[...]
        top, summed, acc = top_in[:, :1], sum_in[:, :1], acc_in[...]
    blocks, outs = refs[:count], refs[count:]
    for first in range(0, count, group):
        keys = [block[...] for block in blocks[first : first + group]]
        scores = [
            lax.dot_general(query, key, ROW_DOT, preferred_element_type=jnp.float32)
            for key in keys
        ]
        ceiling = scores[0].max(-1, keepdims=True)
        for score in scores[1:]:
            ceiling = jnp.maximum(ceiling, score.max(-1, keepdims=True))
        if top is not None:
            ceiling = jnp.maximum(ceiling, top)
        weights = [jnp.exp2(score - ceiling) for score in scores]
        new_sum = sum(weight.sum(-1, keepdims=True) for weight in weights)
        new_acc = sum(
            jnp.dot(weight.astype(jnp.bfloat16), key, preferred_element_type=jnp.float32)
            for weight, key in zip(weights, keys)
        )
        if top is not None:
            shrink = jnp.exp2(top - ceiling)
            new_sum = summed * shrink + new_sum
            new_acc = acc * shrink + new_acc
        top, summed, acc = ceiling, new_sum, new_acc
    if end:
        share_out, level_out = outs
        share_out[...] = (acc / summed).astype(jnp.bfloat16)
        level_out[...] = jnp.broadcast_to(top + jnp.log2(summed), level_out.shape)
        return
    if start:
        outs[0][...] = query
        outs = outs[1:]
    acc_out, top_out, sum_out = outs
    acc_out[...] = acc
    top_out[...] = jnp.broadcast_to(top, top_out.shape)
    sum_out[...] = jnp.broadcast_to(summed, sum_out.shape)


def attend(source, blocks, group=2, start=False, end=False):
    rows = source[0].shape[0]
    keys = sum(block.shape[0] for block in blocks)
    operands = [*source, *blocks]
    bf16 = jax.ShapeDtypeStruct((rows, C), jnp.bfloat16)
    column = jax.ShapeDtypeStruct((rows, 128), jnp.float32)
    outs = (jax.ShapeDtypeStruct((rows, C), jnp.float32), column, column)
    if end:
        outs = (bf16, column)
    elif start:
        outs = (bf16, *outs)
    return pl.pallas_call(
        functools.partial(attend_kernel, len(blocks), group, start, end),
        out_shape=outs,
        in_specs=[VMEM] * len(operands),
        out_specs=tuple(VMEM for _ in outs),
        compiler_params=PARAMS,
        cost_estimate=pl.CostEstimate(
            flops=4 * rows * keys * C, bytes_accessed=2 * keys * C, transcendentals=rows * keys
        ),
    )(*operands)


def finish_kernel(
    acc_ref, top_ref, sum_ref, other_ref, level_ref, state_ref, value_ref, outw_ref, out_ref, field
):
    own = top_ref[:, :1] + jnp.log2(sum_ref[:, :1])
    other = level_ref[...]
    ceiling = jnp.maximum(own, other)
    own_part = jnp.exp2(own - ceiling)
    other_part = jnp.exp2(other - ceiling)
    mixed = acc_ref[...] * (own_part / sum_ref[:, :1]) + other_ref[...].astype(jnp.float32) * (
        other_part
    )
    mixed = (mixed / (own_part + other_part)).astype(jnp.bfloat16)
    attended = jnp.dot(mixed, value_ref[...], preferred_element_type=jnp.float32)
    result = jnp.dot(
        attended.astype(jnp.bfloat16), outw_ref[...], preferred_element_type=jnp.float32
    ) + state_ref[...].astype(jnp.float32)
    for block in range(FRAMES):
        for row in range(ROWS):
            start = (block * ROWS + row) * OWN
            field[row, block * OWN : block * OWN + OWN, :] = result[start : start + OWN, :]
    out_ref[0] = field[...].astype(jnp.bfloat16)


def finish(state, other, level, flat, value_weight, out_weight):
    return pl.pallas_call(
        finish_kernel,
        out_shape=jax.ShapeDtypeStruct((1, ROWS, COLS, C), jnp.bfloat16),
        in_specs=[VMEM] * 8,
        out_specs=VMEM,
        scratch_shapes=[pltpu.VMEM((ROWS, COLS, C), jnp.float32)],
        compiler_params=PARAMS,
    )(*state, other, level, flat, value_weight, out_weight)


def row_halos(field):
    tile = lax.axis_index("tile")
    even = tile % 2 == 0
    top, bottom = field[:, :WIDE, :], field[:, (ROWS - 1) * WIDE :, :]
    far = send(jnp.where(even, top, bottom), NEXT_CHIP)
    near = send(jnp.where(even, bottom, top), CORE)
    far = jnp.where((tile == 0) | (tile == 15), jnp.bfloat16(0), far)
    return jnp.where(even, far, near), jnp.where(even, near, far)


def body(
    latent,
    norm1_gain,
    conv1_weight,
    norm2_gain,
    conv2_weight,
    attn_gain,
    query_weight,
    key_weight,
    value_weight,
    out_weight,
):
    field = lax.all_to_all(pack(latent), "frame", 0, 0)
    conv_one = convolve(field, norm1_gain, conv1_weight)
    column = lax.broadcasted_iota(jnp.int32, (1, ROWS, WIDE, 1), 2).reshape(1, COUNT, 1)
    column = column + (OWN * lax.axis_index("frame") - 1)
    conv_one = jnp.where((column >= 0) & (column < COLS), conv_one, jnp.bfloat16(0))
    hstate = convolve(conv_one, norm2_gain, conv2_weight, field)
    flat = lax.all_to_all(hstate, "frame", 0, 0).reshape(FRAMES * POS, C)
    normed = norm_gain(flat.astype(jnp.float32), attn_gain).astype(jnp.bfloat16)
    half = normed.shape[0] // 2
    low, high = normed[:half], normed[half:]
    behind_low = send(low, UP_X)
    ahead_high = send(high, DOWN_X)
    across = send(normed, OTHER_Z)
    mate = send(normed, CORE)
    normed, mate, low, high = lax.optimization_barrier((normed, mate, low, high))
    behind_high = send(high, UP_X)
    ahead_low = send(low, DOWN_X)
    own = attend([normed, query_weight, key_weight], [normed, mate], start=True)
    (behind_low, ahead_high, own) = lax.optimization_barrier((behind_low, ahead_high, own))
    far_low = send(behind_low, UP_X)
    far_high = send(ahead_high, DOWN_X)
    early = jnp.concatenate([behind_low, ahead_high], 0)
    late = jnp.concatenate([behind_high, ahead_low], 0)
    near_mate = send(jnp.concatenate([early, late], 0), CORE)
    other_query, *other = attend(
        [across, query_weight, key_weight], [mate, early, late], start=True
    )
    (far_low, far_high, other) = lax.optimization_barrier((far_low, far_high, other))
    far = jnp.concatenate([far_low, far_high], 0)
    far_mate = send(far, CORE)
    other = attend([other_query, *other], [near_mate])
    share, level = attend([other_query, *other], [far, far_mate], end=True)
    share_back = send(share, OTHER_Z)
    level_back = send(level[:, 0], OTHER_Z)
    own = lax.optimization_barrier((own, share))[0]
    own = attend(own, [across, early, late, near_mate, far, far_mate])
    return finish(own, share_back, level_back.reshape(-1, 1), flat, value_weight, out_weight)


def solution(mesh):
    return jax.shard_map(
        body,
        mesh=mesh,
        in_specs=(P("frame", "tile", None, None), P(), P(), P(), P(), P(), P(), P(), P(), P()),
        out_specs=P("frame", "tile", None, None),
        check_vma=False,
    )
```

```python
import functools
import math

import jax
import jax.numpy as jnp
from jax import lax
from jax.experimental import pallas as pl
from jax.experimental.pallas import tpu as pltpu
from jax.sharding import PartitionSpec as P

C = 384
FRAMES = 8
ROWS = 4
COLS = 160
OWN = COLS // FRAMES
WIDE = OWN + 4
POS = ROWS * OWN
TILE = FRAMES * POS
BOTH = ("frame", "tile")
VMEM = pl.BlockSpec(memory_space=pltpu.VMEM)
PARAMS = pltpu.CompilerParams(vmem_limit_bytes=24 * 2**20)
CONV_PARAMS = pltpu.CompilerParams(vmem_limit_bytes=28 * 2**20)
STREAM_PARAMS = pltpu.CompilerParams(vmem_limit_bytes=34 * 2**20)
ROW_DOT = (((1,), (1,)), ((), ()))


def coords(device):
    frame, tile = divmod(device, 16)
    return frame, tile // 4, tile // 2 % 2, tile % 2


def permutation(move):
    pairs = []
    for device in range(128):
        frame, x, z, core = move(*coords(device))
        pairs.append((device, frame * 16 + x % 4 * 4 + z % 2 * 2 + core % 2))
    return pairs


CORE = permutation(lambda f, x, z, c: (f, x, z, c + 1))
UP_X = permutation(lambda f, x, z, c: (f, x + 1, z, c))
DOWN_X = permutation(lambda f, x, z, c: (f, x - 1, z, c))
OTHER_Z = permutation(lambda f, x, z, c: (f, x, z + 1, c))

NEXT_CHIP = [
    (f * 16 + i, f * 16 + (i + (1 if i % 2 else 15)) % 16) for f in range(FRAMES) for i in range(16)
]


def send(value, pairs):
    return lax.ppermute(value, BOTH, pairs)


def norm_gain(field, gain):
    squares = jnp.mean(field * field, axis=-1, keepdims=True)
    return field * lax.rsqrt(squares + 1e-06) * gain.astype(jnp.float32)


def silu(u):
    return u / (1.0 + jnp.exp(-u))


def pack_kernel(latent_ref, out_ref, field):
    field[:, 0:8, :] = jnp.zeros((ROWS, 8, C), jnp.float32)
    field[:, COLS + 8 : COLS + 16, :] = jnp.zeros((ROWS, 8, C), jnp.float32)
    field[:, 8 : COLS + 8, :] = latent_ref[0].astype(jnp.float32)
    for block in range(FRAMES):
        start = 6 + OWN * block
        piece = field[:, start : start + WIDE, :]
        out_ref[block] = piece.reshape(ROWS * WIDE, C).astype(jnp.bfloat16)


def pack(latent):
    return pl.pallas_call(
        pack_kernel,
        out_shape=jax.ShapeDtypeStruct((FRAMES, ROWS * WIDE, C), jnp.bfloat16),
        in_specs=[VMEM],
        out_specs=VMEM,
        scratch_shapes=[pltpu.VMEM((ROWS, COLS + 16, C), jnp.float32)],
        compiler_params=PARAMS,
    )(latent)


COUNT = ROWS * WIDE


def activate(value, gain_ref):
    return silu(norm_gain(value, gain_ref[...].reshape(1, 1, C)))


def time_taps(weight_ref, taps, times):
    return jnp.concatenate([weight_ref[time, taps, :] for time in times], 1)


def own_rows_kernel(streamed, main_ref, gain_ref, weight_ref, total_ref, field, stacked, *refs):
    if streamed:
        source, (weight_ref, arrived) = weight_ref, refs
        copies = []
        for time in range(3):
            for part in range(4):
                rows = pl.ds(part * 864, 864)
                copies.append(
                    pltpu.make_async_copy(
                        source.at[time, rows], weight_ref.at[time, rows], arrived.at[time, part]
                    )
                )
        for copy in copies:
            copy.start()
    field[:, :, WIDE:, :] = jnp.zeros((FRAMES, ROWS + 2, 8, C), jnp.float32)
    field[:, 0:1, 0:WIDE, :] = jnp.zeros((FRAMES, 1, WIDE, C), jnp.float32)
    field[:, ROWS + 1 :, 0:WIDE, :] = jnp.zeros((FRAMES, 1, WIDE, C), jnp.float32)

    for t in range(FRAMES):
        main = main_ref[t].astype(jnp.float32).reshape(ROWS, WIDE, C)
        field[t, 1 : ROWS + 1, 0:WIDE, :] = activate(main, gain_ref)
        for dh in range(3):
            for dw in range(3):
                piece = field[t, dh : dh + ROWS, dw : dw + WIDE, :]
                lanes = (dh * 3 + dw) * C
                stacked[t * COUNT : t * COUNT + COUNT, lanes : lanes + C] = piece.reshape(
                    COUNT, C
                ).astype(jnp.bfloat16)
    if streamed:
        for copy in copies:
            copy.wait()
    pair = time_taps(weight_ref, slice(0, 9 * C), (2, 1))
    both = jnp.dot(stacked[...], pair, preferred_element_type=jnp.float32)
    total_ref[...] = both[:, :C]
    total_ref[COUNT:, :] += both[: 7 * COUNT, C:]
    total_ref[2 * COUNT :, :] += jnp.dot(
        stacked[: 6 * COUNT, :],
        time_taps(weight_ref, slice(0, 9 * C), (0,)),
        preferred_element_type=jnp.float32,
    )


def edge_rows_kernel(add, total_ref, above_ref, below_ref, gain_ref, weight_ref, *refs):
    if add:
        latent_ref, out_ref, field, stacked, edge, shifted, trimmed = refs
    else:
        out_ref, field, stacked, edge = refs
    for side, rows_ref in enumerate((above_ref, below_ref)):
        field[side, :, WIDE:, :] = jnp.zeros((FRAMES, 8, C), jnp.float32)
        field[side, :, 0:WIDE, :] = activate(rows_ref[...].astype(jnp.float32), gain_ref)
        for dw in range(3):
            piece = field[side, :, dw : dw + WIDE, :]
            stacked[side, :, dw * C : dw * C + C] = piece.reshape(FRAMES * WIDE, C).astype(
                jnp.bfloat16
            )
        taps = slice(side * 6 * C, side * 6 * C + 3 * C)
        weights = time_taps(weight_ref, taps, (2, 1, 0))
        three = jnp.dot(stacked[side], weights, preferred_element_type=jnp.float32)
        edge[side] = three[:, :C]
        edge[side, WIDE:, :] += three[: 7 * WIDE, C : 2 * C]
        edge[side, 2 * WIDE :, :] += three[: 6 * WIDE, 2 * C :]
    for t in range(FRAMES):
        value = total_ref[t * COUNT : t * COUNT + COUNT, :]
        rows = slice(t * WIDE, t * WIDE + WIDE)
        value = jnp.concatenate(
            [
                value[:WIDE] + edge[0, rows, :],
                value[WIDE : 3 * WIDE],
                value[3 * WIDE :] + edge[1, rows, :],
            ],
            0,
        )
        if not add:
            out_ref[t] = value.astype(jnp.bfloat16)
            continue
        shifted[:, 8 : WIDE + 8, :] = latent_ref[t].astype(jnp.float32).reshape(ROWS, WIDE, C)
        value = value.reshape(ROWS, WIDE, C)[:, :OWN, :] + shifted[:, 10 : OWN + 10, :]
        for row in range(ROWS):
            trimmed[row * OWN : row * OWN + OWN, :] = value[row]
        out_ref[t] = trimmed[...].astype(jnp.bfloat16)


def convolve(main, gain, weight, latent=None):
    add = latent is not None
    gain = gain.reshape(1, C)
    above, below = row_halos(main)
    streamed = not add
    total = pl.pallas_call(
        functools.partial(own_rows_kernel, streamed),
        out_shape=jax.ShapeDtypeStruct((FRAMES * COUNT, C), jnp.float32),
        in_specs=[VMEM, VMEM, pl.BlockSpec(memory_space=pltpu.HBM) if streamed else VMEM],
        out_specs=VMEM,
        scratch_shapes=[
            pltpu.VMEM((FRAMES, ROWS + 2, WIDE + 8, C), jnp.float32),
            pltpu.VMEM((FRAMES * COUNT, 9 * C), jnp.bfloat16),
        ]
        + streamed * [pltpu.VMEM((3, 9 * C, C), jnp.bfloat16), pltpu.SemaphoreType.DMA((3, 4))],
        compiler_params=STREAM_PARAMS if streamed else CONV_PARAMS,
        cost_estimate=pl.CostEstimate(
            flops=2 * 768 * 27 * C * C, bytes_accessed=27 * C * C * 2, transcendentals=10**6
        ),
    )(main, gain, pltpu.with_memory_space_constraint(weight, pltpu.HBM) if streamed else weight)
    operands = [total, above, below, gain, weight]
    scratch = [
        pltpu.VMEM((2, FRAMES, WIDE + 8, C), jnp.float32),
        pltpu.VMEM((2, FRAMES * WIDE, 3 * C), jnp.bfloat16),
        pltpu.VMEM((2, FRAMES * WIDE, C), jnp.float32),
    ]
    if add:
        operands.append(latent)
        scratch.append(pltpu.VMEM((ROWS, WIDE + 8, C), jnp.float32))
        scratch.append(pltpu.VMEM((POS, C), jnp.float32))
    return pl.pallas_call(
        functools.partial(edge_rows_kernel, add),
        out_shape=jax.ShapeDtypeStruct((FRAMES, POS if add else COUNT, C), jnp.bfloat16),
        in_specs=[VMEM] * len(operands),
        out_specs=VMEM,
        scratch_shapes=scratch,
        compiler_params=CONV_PARAMS,
        cost_estimate=pl.CostEstimate(
            flops=2 * 384 * 9 * C * C, bytes_accessed=27 * C * C * 2, transcendentals=10**5
        ),
    )(*operands)


def attend_kernel(count, group, start, end, *refs):
    if start:
        rows_ref, query_weight_ref, key_weight_ref = refs[:3]
        refs = refs[3:]
        scale = math.log2(math.e) / math.sqrt(C)
        query = jnp.dot(
            rows_ref[...], query_weight_ref[...], preferred_element_type=jnp.float32
        ).astype(jnp.bfloat16)
        query = lax.dot_general(
            query, key_weight_ref[...], ROW_DOT, preferred_element_type=jnp.float32
        )
        query = (query * scale).astype(jnp.bfloat16)
        top = summed = acc = None
    else:
        query_ref, acc_in, top_in, sum_in = refs[:4]
        refs = refs[4:]
        query = query_ref[...]
        top, summed, acc = top_in[:, :1], sum_in[:, :1], acc_in[...]
    blocks, outs = refs[:count], refs[count:]
    parts = [
        block[first : first + TILE, :]
        for block in blocks
        for first in range(0, block.shape[0], TILE)
    ]
    keys = [
        parts[first] if group == 1 else jnp.concatenate(parts[first : first + group], 0)
        for first in range(0, len(parts), group)
    ]

    def score(key):
        return lax.dot_general(query, key, ROW_DOT, preferred_element_type=jnp.float32)

    following = score(keys[0])
    for index, key in enumerate(keys):
        scores = following
        if index + 1 < len(keys):
            following = score(keys[index + 1])
        ceiling = scores.max(-1, keepdims=True)
        if top is not None:
            ceiling = jnp.maximum(ceiling, top)
        weights = jnp.exp2(scores - ceiling)
        new_sum = weights.sum(-1, keepdims=True)
        new_acc = jnp.dot(weights.astype(jnp.bfloat16), key, preferred_element_type=jnp.float32)
        if top is not None:
            shrink = jnp.exp2(top - ceiling)
            new_sum = summed * shrink + new_sum
            new_acc = acc * shrink + new_acc
        top, summed, acc = ceiling, new_sum, new_acc
    if end:
        share_out, level_out = outs
        share_out[...] = (acc / summed).astype(jnp.bfloat16)
        level_out[...] = jnp.broadcast_to(top + jnp.log2(summed), level_out.shape)
        return
    if start:
        outs[0][...] = query
        outs = outs[1:]
    acc_out, top_out, sum_out = outs
    acc_out[...] = acc
    top_out[...] = jnp.broadcast_to(top, top_out.shape)
    sum_out[...] = jnp.broadcast_to(summed, sum_out.shape)


def attend(source, blocks, group=1, start=False, end=False):
    rows = source[0].shape[0]
    keys = sum(block.shape[0] for block in blocks)
    operands = [*source, *blocks]
    bf16 = jax.ShapeDtypeStruct((rows, C), jnp.bfloat16)
    column = jax.ShapeDtypeStruct((rows, 128), jnp.float32)
    outs = (jax.ShapeDtypeStruct((rows, C), jnp.float32), column, column)
    if end:
        outs = (bf16, column)
    elif start:
        outs = (bf16, *outs)
    return pl.pallas_call(
        functools.partial(attend_kernel, len(blocks), group, start, end),
        out_shape=outs,
        in_specs=[VMEM] * len(operands),
        out_specs=tuple(VMEM for _ in outs),
        compiler_params=PARAMS,
        cost_estimate=pl.CostEstimate(
            flops=4 * rows * keys * C, bytes_accessed=2 * keys * C, transcendentals=rows * keys
        ),
    )(*operands)


def finish_kernel(
    acc_ref, top_ref, sum_ref, other_ref, level_ref, state_ref, value_ref, outw_ref, out_ref, field
):
    own = top_ref[:, :1] + jnp.log2(sum_ref[:, :1])
    other = level_ref[...]
    ceiling = jnp.maximum(own, other)
    own_part = jnp.exp2(own - ceiling)
    other_part = jnp.exp2(other - ceiling)
    mixed = acc_ref[...] * (own_part / sum_ref[:, :1]) + other_ref[...].astype(jnp.float32) * (
        other_part
    )
    mixed = (mixed / (own_part + other_part)).astype(jnp.bfloat16)
    attended = jnp.dot(mixed, value_ref[...], preferred_element_type=jnp.float32)
    result = jnp.dot(
        attended.astype(jnp.bfloat16), outw_ref[...], preferred_element_type=jnp.float32
    ) + state_ref[...].astype(jnp.float32)
    for block in range(FRAMES):
        for row in range(ROWS):
            start = (block * ROWS + row) * OWN
            field[row, block * OWN : block * OWN + OWN, :] = result[start : start + OWN, :]
    out_ref[0] = field[...].astype(jnp.bfloat16)


def finish(state, other, level, flat, value_weight, out_weight):
    return pl.pallas_call(
        finish_kernel,
        out_shape=jax.ShapeDtypeStruct((1, ROWS, COLS, C), jnp.bfloat16),
        in_specs=[VMEM] * 8,
        out_specs=VMEM,
        scratch_shapes=[pltpu.VMEM((ROWS, COLS, C), jnp.float32)],
        compiler_params=PARAMS,
    )(*state, other, level, flat, value_weight, out_weight)


def row_halos(field):
    tile = lax.axis_index("tile")
    even = tile % 2 == 0
    top, bottom = field[:, :WIDE, :], field[:, (ROWS - 1) * WIDE :, :]
    far = send(jnp.where(even, top, bottom), NEXT_CHIP)
    near = send(jnp.where(even, bottom, top), CORE)
    far = jnp.where((tile == 0) | (tile == 15), jnp.bfloat16(0), far)
    return jnp.where(even, far, near), jnp.where(even, near, far)


def body(
    latent,
    norm1_gain,
    conv1_weight,
    norm2_gain,
    conv2_weight,
    attn_gain,
    query_weight,
    key_weight,
    value_weight,
    out_weight,
):
    field = lax.all_to_all(pack(latent), "frame", 0, 0)
    conv_one = convolve(field, norm1_gain, conv1_weight.reshape(3, 9 * C, C))
    column = lax.broadcasted_iota(jnp.int32, (1, ROWS, WIDE, 1), 2).reshape(1, COUNT, 1)
    column = column + (OWN * lax.axis_index("frame") - 1)
    conv_one = jnp.where((column >= 0) & (column < COLS), conv_one, jnp.bfloat16(0))
    hstate = convolve(conv_one, norm2_gain, conv2_weight.reshape(3, 9 * C, C), field)
    flat = lax.all_to_all(hstate, "frame", 0, 0).reshape(FRAMES * POS, C)
    normed = norm_gain(flat.astype(jnp.float32), attn_gain).astype(jnp.bfloat16)
    half = TILE // 2
    low, high = normed[:half], normed[half:]
    behind_low = send(low, UP_X)
    ahead_high = send(high, DOWN_X)
    across = send(normed, OTHER_Z)
    mate = send(normed, CORE)
    normed, mate, low, high = lax.optimization_barrier((normed, mate, low, high))
    behind_high = send(high, UP_X)
    ahead_low = send(low, DOWN_X)
    own = attend([normed, query_weight, key_weight], [normed, mate], start=True)
    (behind_low, ahead_high, own) = lax.optimization_barrier((behind_low, ahead_high, own))
    far_low = send(behind_low, UP_X)
    far_high = send(ahead_high, DOWN_X)
    early = jnp.concatenate([behind_low, ahead_high], 0)
    late = jnp.concatenate([behind_high, ahead_low], 0)
    near_mate = send(jnp.concatenate([early, late], 0), CORE)
    other_query, *other = attend(
        [across, query_weight, key_weight], [mate, early, late], start=True
    )
    (far_low, far_high, other) = lax.optimization_barrier((far_low, far_high, other))
    far = jnp.concatenate([far_low, far_high], 0)
    far_mate = send(far, CORE)
    other = attend([other_query, *other], [near_mate])
    share, level = attend([other_query, *other], [far, far_mate], end=True)
    share_back = send(share, OTHER_Z)
    level_back = send(level[:, 0], OTHER_Z)
    own = lax.optimization_barrier((own, share))[0]
    own = attend(own, [across, early, late, near_mate, far, far_mate], group=2)
    return finish(own, share_back, level_back.reshape(-1, 1), flat, value_weight, out_weight)


def solution(mesh):
    return jax.shard_map(
        body,
        mesh=mesh,
        in_specs=(P("frame", "tile", None, None), P(), P(), P(), P(), P(), P(), P(), P(), P()),
        out_specs=P("frame", "tile", None, None),
        check_vma=False,
    )
```

```python
import functools
import math

import jax
import jax.numpy as jnp
from jax import lax
from jax.experimental import pallas as pl
from jax.experimental.pallas import tpu as pltpu
from jax.sharding import PartitionSpec as P

C = 384
FRAMES = 8
ROWS = 4
COLS = 160
OWN = COLS // FRAMES
WIDE = OWN + 4
POS = ROWS * OWN
TILE = FRAMES * POS
BOTH = ("frame", "tile")
VMEM = pl.BlockSpec(memory_space=pltpu.VMEM)
PARAMS = pltpu.CompilerParams(vmem_limit_bytes=24 * 2**20)
CONV_PARAMS = pltpu.CompilerParams(vmem_limit_bytes=28 * 2**20)
STREAM_PARAMS = pltpu.CompilerParams(vmem_limit_bytes=34 * 2**20)
ROW_DOT = (((1,), (1,)), ((), ()))


def coords(device):
    frame, tile = divmod(device, 16)
    return frame, tile // 4, tile // 2 % 2, tile % 2


def permutation(move):
    pairs = []
    for device in range(128):
        frame, x, z, core = move(*coords(device))
        pairs.append((device, frame * 16 + x % 4 * 4 + z % 2 * 2 + core % 2))
    return pairs


CORE = permutation(lambda f, x, z, c: (f, x, z, c + 1))
UP_X = permutation(lambda f, x, z, c: (f, x + 1, z, c))
DOWN_X = permutation(lambda f, x, z, c: (f, x - 1, z, c))
OTHER_Z = permutation(lambda f, x, z, c: (f, x, z + 1, c))

NEXT_CHIP = [
    (f * 16 + i, f * 16 + (i + (1 if i % 2 else 15)) % 16) for f in range(FRAMES) for i in range(16)
]


def send(value, pairs):
    return lax.ppermute(value, BOTH, pairs)


def norm_gain(field, gain):
    squares = jnp.mean(field * field, axis=-1, keepdims=True)
    return field * lax.rsqrt(squares + 1e-06) * gain.astype(jnp.float32)


def silu(u):
    return u / (1.0 + jnp.exp(-u))


def pack_kernel(latent_ref, out_ref, field):
    field[:, 0:8, :] = jnp.zeros((ROWS, 8, C), jnp.float32)
    field[:, COLS + 8 : COLS + 16, :] = jnp.zeros((ROWS, 8, C), jnp.float32)
    field[:, 8 : COLS + 8, :] = latent_ref[0].astype(jnp.float32)
    for block in range(FRAMES):
        start = 6 + OWN * block
        piece = field[:, start : start + WIDE, :]
        out_ref[block] = piece.reshape(ROWS * WIDE, C).astype(jnp.bfloat16)


def pack(latent):
    return pl.pallas_call(
        pack_kernel,
        out_shape=jax.ShapeDtypeStruct((FRAMES, ROWS * WIDE, C), jnp.bfloat16),
        in_specs=[VMEM],
        out_specs=VMEM,
        scratch_shapes=[pltpu.VMEM((ROWS, COLS + 16, C), jnp.float32)],
        compiler_params=PARAMS,
    )(latent)


COUNT = ROWS * WIDE


def activate(value, gain_ref):
    return silu(norm_gain(value, gain_ref[...].reshape(1, 1, C)))


def time_taps(weight_ref, taps, times):
    return jnp.concatenate([weight_ref[time, taps, :] for time in times], 1)


def own_rows_kernel(streamed, main_ref, gain_ref, weight_ref, total_ref, field, stacked, *refs):
    if streamed:
        source, (weight_ref, arrived) = weight_ref, refs
        copies = []
        for time in range(3):
            for part in range(4):
                rows = pl.ds(part * 864, 864)
                copies.append(
                    pltpu.make_async_copy(
                        source.at[time, rows], weight_ref.at[time, rows], arrived.at[time, part]
                    )
                )
        for copy in copies:
            copy.start()
    field[:, :, WIDE:, :] = jnp.zeros((FRAMES, ROWS + 2, 8, C), jnp.float32)
    field[:, 0:1, 0:WIDE, :] = jnp.zeros((FRAMES, 1, WIDE, C), jnp.float32)
    field[:, ROWS + 1 :, 0:WIDE, :] = jnp.zeros((FRAMES, 1, WIDE, C), jnp.float32)

    for t in range(FRAMES):
        main = main_ref[t].astype(jnp.float32).reshape(ROWS, WIDE, C)
        field[t, 1 : ROWS + 1, 0:WIDE, :] = activate(main, gain_ref)
        for dh in range(3):
            for dw in range(3):
                piece = field[t, dh : dh + ROWS, dw : dw + WIDE, :]
                lanes = (dh * 3 + dw) * C
                stacked[t * COUNT : t * COUNT + COUNT, lanes : lanes + C] = piece.reshape(
                    COUNT, C
                ).astype(jnp.bfloat16)
    if streamed:
        for copy in copies:
            copy.wait()
    pair = time_taps(weight_ref, slice(0, 9 * C), (2, 1))
    both = jnp.dot(stacked[...], pair, preferred_element_type=jnp.float32)
    total_ref[...] = both[:, :C]
    total_ref[COUNT:, :] += both[: 7 * COUNT, C:]
    total_ref[2 * COUNT :, :] += jnp.dot(
        stacked[: 6 * COUNT, :],
        time_taps(weight_ref, slice(0, 9 * C), (0,)),
        preferred_element_type=jnp.float32,
    )


def edge_rows_kernel(add, total_ref, above_ref, below_ref, gain_ref, weight_ref, *refs):
    if add:
        latent_ref, out_ref, field, stacked, edge, shifted, trimmed = refs
    else:
        out_ref, field, stacked, edge = refs
    for side, rows_ref in enumerate((above_ref, below_ref)):
        field[side, :, WIDE:, :] = jnp.zeros((FRAMES, 8, C), jnp.float32)
        field[side, :, 0:WIDE, :] = activate(rows_ref[...].astype(jnp.float32), gain_ref)
        for dw in range(3):
            piece = field[side, :, dw : dw + WIDE, :]
            stacked[side, :, dw * C : dw * C + C] = piece.reshape(FRAMES * WIDE, C).astype(
                jnp.bfloat16
            )
        taps = slice(side * 6 * C, side * 6 * C + 3 * C)
        weights = time_taps(weight_ref, taps, (2, 1, 0))
        three = jnp.dot(stacked[side], weights, preferred_element_type=jnp.float32)
        edge[side] = three[:, :C]
        edge[side, WIDE:, :] += three[: 7 * WIDE, C : 2 * C]
        edge[side, 2 * WIDE :, :] += three[: 6 * WIDE, 2 * C :]
    for t in range(FRAMES):
        value = total_ref[t * COUNT : t * COUNT + COUNT, :]
        rows = slice(t * WIDE, t * WIDE + WIDE)
        value = jnp.concatenate(
            [
                value[:WIDE] + edge[0, rows, :],
                value[WIDE : 3 * WIDE],
                value[3 * WIDE :] + edge[1, rows, :],
            ],
            0,
        )
        if not add:
            out_ref[t] = value.astype(jnp.bfloat16)
            continue
        shifted[:, 8 : WIDE + 8, :] = latent_ref[t].astype(jnp.float32).reshape(ROWS, WIDE, C)
        value = value.reshape(ROWS, WIDE, C)[:, :OWN, :] + shifted[:, 10 : OWN + 10, :]
        for row in range(ROWS):
            trimmed[row * OWN : row * OWN + OWN, :] = value[row]
        out_ref[t] = trimmed[...].astype(jnp.bfloat16)


def convolve(main, gain, weight, latent=None):
    add = latent is not None
    gain = gain.reshape(1, C)
    above, below = row_halos(main)
    streamed = not add
    total = pl.pallas_call(
        functools.partial(own_rows_kernel, streamed),
        out_shape=jax.ShapeDtypeStruct((FRAMES * COUNT, C), jnp.float32),
        in_specs=[VMEM, VMEM, pl.BlockSpec(memory_space=pltpu.HBM) if streamed else VMEM],
        out_specs=VMEM,
        scratch_shapes=[
            pltpu.VMEM((FRAMES, ROWS + 2, WIDE + 8, C), jnp.float32),
            pltpu.VMEM((FRAMES * COUNT, 9 * C), jnp.bfloat16),
        ]
        + streamed * [pltpu.VMEM((3, 9 * C, C), jnp.bfloat16), pltpu.SemaphoreType.DMA((3, 4))],
        compiler_params=STREAM_PARAMS if streamed else CONV_PARAMS,
        cost_estimate=pl.CostEstimate(
            flops=2 * 768 * 27 * C * C, bytes_accessed=27 * C * C * 2, transcendentals=10**6
        ),
    )(main, gain, pltpu.with_memory_space_constraint(weight, pltpu.HBM) if streamed else weight)
    operands = [total, above, below, gain, weight]
    scratch = [
        pltpu.VMEM((2, FRAMES, WIDE + 8, C), jnp.float32),
        pltpu.VMEM((2, FRAMES * WIDE, 3 * C), jnp.bfloat16),
        pltpu.VMEM((2, FRAMES * WIDE, C), jnp.float32),
    ]
    if add:
        operands.append(latent)
        scratch.append(pltpu.VMEM((ROWS, WIDE + 8, C), jnp.float32))
        scratch.append(pltpu.VMEM((POS, C), jnp.float32))
    return pl.pallas_call(
        functools.partial(edge_rows_kernel, add),
        out_shape=jax.ShapeDtypeStruct((FRAMES, POS if add else COUNT, C), jnp.bfloat16),
        in_specs=[VMEM] * len(operands),
        out_specs=VMEM,
        scratch_shapes=scratch,
        compiler_params=CONV_PARAMS,
        cost_estimate=pl.CostEstimate(
            flops=2 * 384 * 9 * C * C, bytes_accessed=27 * C * C * 2, transcendentals=10**5
        ),
    )(*operands)


def attend_kernel(count, group, start, end, *refs):
    if start:
        rows_ref, query_weight_ref, key_weight_ref = refs[:3]
        refs = refs[3:]
        scale = math.log2(math.e) / math.sqrt(C)
        query = jnp.dot(
            rows_ref[...], query_weight_ref[...], preferred_element_type=jnp.float32
        ).astype(jnp.bfloat16)
        query = lax.dot_general(
            query, key_weight_ref[...], ROW_DOT, preferred_element_type=jnp.float32
        )
        query = (query * scale).astype(jnp.bfloat16)
        top = summed = acc = None
    else:
        query_ref, acc_in, top_in, sum_in = refs[:4]
        refs = refs[4:]
        query = query_ref[...]
        top, summed, acc = top_in[:, :1], sum_in[:, :1], acc_in[...]
    blocks, outs = refs[:count], refs[count:]
    parts = [
        block[first : first + TILE, :]
        for block in blocks
        for first in range(0, block.shape[0], TILE)
    ]
    keys = [
        parts[first] if group == 1 else jnp.concatenate(parts[first : first + group], 0)
        for first in range(0, len(parts), group)
    ]

    def score(key):
        return lax.dot_general(query, key, ROW_DOT, preferred_element_type=jnp.float32)

    following = score(keys[0])
    for index, key in enumerate(keys):
        scores = following
        if index + 1 < len(keys):
            following = score(keys[index + 1])
        ceiling = scores.max(-1, keepdims=True)
        if top is not None:
            ceiling = jnp.maximum(ceiling, top)
        weights = jnp.exp2(scores - ceiling)
        new_sum = weights.sum(-1, keepdims=True)
        new_acc = jnp.dot(weights.astype(jnp.bfloat16), key, preferred_element_type=jnp.float32)
        if top is not None:
            shrink = jnp.exp2(top - ceiling)
            new_sum = summed * shrink + new_sum
            new_acc = acc * shrink + new_acc
        top, summed, acc = ceiling, new_sum, new_acc
    if end:
        share_out, level_out = outs
        share_out[...] = (acc / summed).astype(jnp.bfloat16)
        level_out[...] = jnp.broadcast_to(top + jnp.log2(summed), level_out.shape)
        return
    if start:
        outs[0][...] = query
        outs = outs[1:]
    acc_out, top_out, sum_out = outs
    acc_out[...] = acc
    top_out[...] = jnp.broadcast_to(top, top_out.shape)
    sum_out[...] = jnp.broadcast_to(summed, sum_out.shape)


def attend(source, blocks, group=1, start=False, end=False):
    rows = source[0].shape[0]
    keys = sum(block.shape[0] for block in blocks)
    operands = [*source, *blocks]
    bf16 = jax.ShapeDtypeStruct((rows, C), jnp.bfloat16)
    column = jax.ShapeDtypeStruct((rows, 128), jnp.float32)
    outs = (jax.ShapeDtypeStruct((rows, C), jnp.float32), column, column)
    if end:
        outs = (bf16, column)
    elif start:
        outs = (bf16, *outs)
    return pl.pallas_call(
        functools.partial(attend_kernel, len(blocks), group, start, end),
        out_shape=outs,
        in_specs=[VMEM] * len(operands),
        out_specs=tuple(VMEM for _ in outs),
        compiler_params=PARAMS,
        cost_estimate=pl.CostEstimate(
            flops=4 * rows * keys * C, bytes_accessed=2 * keys * C, transcendentals=rows * keys
        ),
    )(*operands)


def finish_kernel(
    acc_ref, top_ref, sum_ref, other_ref, level_ref, state_ref, value_ref, outw_ref, out_ref, field
):
    own = top_ref[:, :1] + jnp.log2(sum_ref[:, :1])
    other = level_ref[...]
    ceiling = jnp.maximum(own, other)
    own_part = jnp.exp2(own - ceiling)
    other_part = jnp.exp2(other - ceiling)
    mixed = acc_ref[...] * (own_part / sum_ref[:, :1]) + other_ref[...].astype(jnp.float32) * (
        other_part
    )
    mixed = (mixed / (own_part + other_part)).astype(jnp.bfloat16)
    attended = jnp.dot(mixed, value_ref[...], preferred_element_type=jnp.float32)
    result = jnp.dot(
        attended.astype(jnp.bfloat16), outw_ref[...], preferred_element_type=jnp.float32
    ) + state_ref[...].astype(jnp.float32)
    for block in range(FRAMES):
        for row in range(ROWS):
            start = (block * ROWS + row) * OWN
            field[row, block * OWN : block * OWN + OWN, :] = result[start : start + OWN, :]
    out_ref[0] = field[...].astype(jnp.bfloat16)


def finish(state, other, level, flat, value_weight, out_weight):
    return pl.pallas_call(
        finish_kernel,
        out_shape=jax.ShapeDtypeStruct((1, ROWS, COLS, C), jnp.bfloat16),
        in_specs=[VMEM] * 8,
        out_specs=VMEM,
        scratch_shapes=[pltpu.VMEM((ROWS, COLS, C), jnp.float32)],
        compiler_params=PARAMS,
    )(*state, other, level, flat, value_weight, out_weight)


def row_halos(field):
    tile = lax.axis_index("tile")
    even = tile % 2 == 0
    top, bottom = field[:, :WIDE, :], field[:, (ROWS - 1) * WIDE :, :]
    far = send(jnp.where(even, top, bottom), NEXT_CHIP)
    near = send(jnp.where(even, bottom, top), CORE)
    far = jnp.where((tile == 0) | (tile == 15), jnp.bfloat16(0), far)
    return jnp.where(even, far, near), jnp.where(even, near, far)


def body(
    latent,
    norm1_gain,
    conv1_weight,
    norm2_gain,
    conv2_weight,
    attn_gain,
    query_weight,
    key_weight,
    value_weight,
    out_weight,
):
    field = lax.all_to_all(pack(latent), "frame", 0, 0)
    field, norm1_gain, norm2_gain, conv1_weight, conv2_weight, attn_gain = (
        lax.optimization_barrier(
            (field, norm1_gain, norm2_gain, conv1_weight, conv2_weight, attn_gain)
        )
    )
    conv_one = convolve(field, norm1_gain, conv1_weight.reshape(3, 9 * C, C))
    column = lax.broadcasted_iota(jnp.int32, (1, ROWS, WIDE, 1), 2).reshape(1, COUNT, 1)
    conv_one, column = lax.optimization_barrier((conv_one, column))
    column = column + (OWN * lax.axis_index("frame") - 1)
    conv_one = jnp.where((column >= 0) & (column < COLS), conv_one, jnp.bfloat16(0))
    hstate = convolve(conv_one, norm2_gain, conv2_weight.reshape(3, 9 * C, C), field)
    flat = lax.all_to_all(hstate, "frame", 0, 0).reshape(FRAMES * POS, C)
    flat, attn_gain, query_weight, key_weight, value_weight, out_weight = (
        lax.optimization_barrier(
            (flat, attn_gain, query_weight, key_weight, value_weight, out_weight)
        )
    )
    normed = norm_gain(flat.astype(jnp.float32), attn_gain).astype(jnp.bfloat16)
    half = TILE // 2
    low, high = normed[:half], normed[half:]
    behind_low = send(low, UP_X)
    ahead_high = send(high, DOWN_X)
    across = send(normed, OTHER_Z)
    mate = send(normed, CORE)
    normed, mate, low, high = lax.optimization_barrier((normed, mate, low, high))
    behind_high = send(high, UP_X)
    ahead_low = send(low, DOWN_X)
    own = attend([normed, query_weight, key_weight], [normed, mate], start=True)
    (behind_low, ahead_high, own) = lax.optimization_barrier((behind_low, ahead_high, own))
    far_low = send(behind_low, UP_X)
    far_high = send(ahead_high, DOWN_X)
    early = jnp.concatenate([behind_low, ahead_high], 0)
    late = jnp.concatenate([behind_high, ahead_low], 0)
    near_mate = send(jnp.concatenate([early, late], 0), CORE)
    other_query, *other = attend(
        [across, query_weight, key_weight], [mate, early, late], start=True
    )
    (far_low, far_high, other) = lax.optimization_barrier((far_low, far_high, other))
    far = jnp.concatenate([far_low, far_high], 0)
    far_mate = send(far, CORE)
    other = attend([other_query, *other], [near_mate])
    share, level = attend([other_query, *other], [far, far_mate], end=True)
    share_back = send(share, OTHER_Z)
    level_back = send(level[:, 0], OTHER_Z)
    own = lax.optimization_barrier((own, share))[0]
    own = attend(own, [across, early, late, near_mate, far, far_mate], group=2)
    return finish(own, share_back, level_back.reshape(-1, 1), flat, value_weight, out_weight)


def solution(mesh):
    return jax.shard_map(
        body,
        mesh=mesh,
        in_specs=(P("frame", "tile", None, None), P(), P(), P(), P(), P(), P(), P(), P(), P()),
        out_specs=P("frame", "tile", None, None),
        check_vma=False,
    )
```

```python
import functools
import math

import jax
import jax.numpy as jnp
from jax import lax
from jax.experimental import pallas as pl
from jax.experimental.pallas import tpu as pltpu
from jax.sharding import PartitionSpec as P

C = 384
FRAMES = 8
ROWS = 4
COLS = 160
OWN = COLS // FRAMES
WIDE = OWN + 4
POS = ROWS * OWN
TILE = FRAMES * POS
BOTH = ("frame", "tile")
VMEM = pl.BlockSpec(memory_space=pltpu.VMEM)
PARAMS = pltpu.CompilerParams(vmem_limit_bytes=24 * 2**20)
CONV_PARAMS = pltpu.CompilerParams(vmem_limit_bytes=28 * 2**20)
STREAM_PARAMS = pltpu.CompilerParams(vmem_limit_bytes=34 * 2**20)
ROW_DOT = (((1,), (1,)), ((), ()))


def coords(device):
    frame, tile = divmod(device, 16)
    return frame, tile // 4, tile // 2 % 2, tile % 2


def permutation(move):
    pairs = []
    for device in range(128):
        frame, x, z, core = move(*coords(device))
        pairs.append((device, frame * 16 + x % 4 * 4 + z % 2 * 2 + core % 2))
    return pairs


CORE = permutation(lambda f, x, z, c: (f, x, z, c + 1))
UP_X = permutation(lambda f, x, z, c: (f, x + 1, z, c))
DOWN_X = permutation(lambda f, x, z, c: (f, x - 1, z, c))
OTHER_Z = permutation(lambda f, x, z, c: (f, x, z + 1, c))

NEXT_CHIP = [
    (f * 16 + i, f * 16 + (i + (1 if i % 2 else 15)) % 16) for f in range(FRAMES) for i in range(16)
]


def send(value, pairs):
    return lax.ppermute(value, BOTH, pairs)


def norm_gain(field, gain):
    squares = jnp.mean(field * field, axis=-1, keepdims=True)
    return field * lax.rsqrt(squares + 1e-06) * gain.astype(jnp.float32)


def silu(u):
    return u / (1.0 + jnp.exp(-u))


def pack_kernel(latent_ref, out_ref, field):
    field[:, 0:8, :] = jnp.zeros((ROWS, 8, C), jnp.float32)
    field[:, COLS + 8 : COLS + 16, :] = jnp.zeros((ROWS, 8, C), jnp.float32)
    field[:, 8 : COLS + 8, :] = latent_ref[0].astype(jnp.float32)
    for block in range(FRAMES):
        start = 6 + OWN * block
        piece = field[:, start : start + WIDE, :]
        out_ref[block] = piece.reshape(ROWS * WIDE, C).astype(jnp.bfloat16)


def pack(latent):
    return pl.pallas_call(
        pack_kernel,
        out_shape=jax.ShapeDtypeStruct((FRAMES, ROWS * WIDE, C), jnp.bfloat16),
        in_specs=[VMEM],
        out_specs=VMEM,
        scratch_shapes=[pltpu.VMEM((ROWS, COLS + 16, C), jnp.float32)],
        compiler_params=PARAMS,
    )(latent)


COUNT = ROWS * WIDE


def activate(value, gain_ref):
    return silu(norm_gain(value, gain_ref[...].reshape(1, 1, C)))


def time_taps(weight_ref, taps, times):
    return jnp.concatenate([weight_ref[time, taps, :] for time in times], 1)


def own_rows_kernel(streamed, main_ref, gain_ref, weight_ref, total_ref, field, stacked, *refs):
    if streamed:
        source, (weight_ref, arrived) = weight_ref, refs
        copies = []
        for time in range(3):
            for part in range(4):
                rows = pl.ds(part * 864, 864)
                copies.append(
                    pltpu.make_async_copy(
                        source.at[time, rows], weight_ref.at[time, rows], arrived.at[time, part]
                    )
                )
        for copy in copies:
            copy.start()
    field[:, :, WIDE:, :] = jnp.zeros((FRAMES, ROWS + 2, 8, C), jnp.float32)
    field[:, 0:1, 0:WIDE, :] = jnp.zeros((FRAMES, 1, WIDE, C), jnp.float32)
    field[:, ROWS + 1 :, 0:WIDE, :] = jnp.zeros((FRAMES, 1, WIDE, C), jnp.float32)

    for t in range(FRAMES):
        main = main_ref[t].astype(jnp.float32).reshape(ROWS, WIDE, C)
        field[t, 1 : ROWS + 1, 0:WIDE, :] = activate(main, gain_ref)
        for dh in range(3):
            for dw in range(3):
                piece = field[t, dh : dh + ROWS, dw : dw + WIDE, :]
                lanes = (dh * 3 + dw) * C
                stacked[t * COUNT : t * COUNT + COUNT, lanes : lanes + C] = piece.reshape(
                    COUNT, C
                ).astype(jnp.bfloat16)
    if streamed:
        for copy in copies:
            copy.wait()
    pair = time_taps(weight_ref, slice(0, 9 * C), (2, 1))
    both = jnp.dot(stacked[...], pair, preferred_element_type=jnp.float32)
    total_ref[...] = both[:, :C]
    total_ref[COUNT:, :] += both[: 7 * COUNT, C:]
    total_ref[2 * COUNT :, :] += jnp.dot(
        stacked[: 6 * COUNT, :],
        time_taps(weight_ref, slice(0, 9 * C), (0,)),
        preferred_element_type=jnp.float32,
    )


def edge_rows_kernel(add, total_ref, above_ref, below_ref, gain_ref, weight_ref, *refs):
    if add:
        latent_ref, out_ref, field, stacked, edge, shifted, trimmed = refs
    else:
        first_ref, out_ref, field, stacked, edge = refs
        column = lax.broadcasted_iota(jnp.int32, (ROWS, WIDE, C), 1).reshape(COUNT, C)
        column = column + first_ref[0]
        inside = (column >= 0) & (column < COLS)
    for side, rows_ref in enumerate((above_ref, below_ref)):
        field[side, :, WIDE:, :] = jnp.zeros((FRAMES, 8, C), jnp.float32)
        field[side, :, 0:WIDE, :] = activate(rows_ref[...].astype(jnp.float32), gain_ref)
        for dw in range(3):
            piece = field[side, :, dw : dw + WIDE, :]
            stacked[side, :, dw * C : dw * C + C] = piece.reshape(FRAMES * WIDE, C).astype(
                jnp.bfloat16
            )
        taps = slice(side * 6 * C, side * 6 * C + 3 * C)
        weights = time_taps(weight_ref, taps, (2, 1, 0))
        three = jnp.dot(stacked[side], weights, preferred_element_type=jnp.float32)
        edge[side] = three[:, :C]
        edge[side, WIDE:, :] += three[: 7 * WIDE, C : 2 * C]
        edge[side, 2 * WIDE :, :] += three[: 6 * WIDE, 2 * C :]
    for t in range(FRAMES):
        value = total_ref[t * COUNT : t * COUNT + COUNT, :]
        rows = slice(t * WIDE, t * WIDE + WIDE)
        value = jnp.concatenate(
            [
                value[:WIDE] + edge[0, rows, :],
                value[WIDE : 3 * WIDE],
                value[3 * WIDE :] + edge[1, rows, :],
            ],
            0,
        )
        if not add:
            out_ref[t] = jnp.where(inside, value, 0.0).astype(jnp.bfloat16)
            continue
        shifted[:, 8 : WIDE + 8, :] = latent_ref[t].astype(jnp.float32).reshape(ROWS, WIDE, C)
        value = value.reshape(ROWS, WIDE, C)[:, :OWN, :] + shifted[:, 10 : OWN + 10, :]
        for row in range(ROWS):
            trimmed[row * OWN : row * OWN + OWN, :] = value[row]
        out_ref[t] = trimmed[...].astype(jnp.bfloat16)


def convolve(main, place, gain, weight, latent=None):
    add = latent is not None
    gain = gain.reshape(1, C)
    even, outermost, first_column = place
    above, below = row_halos(main, even, outermost)
    streamed = not add
    total = pl.pallas_call(
        functools.partial(own_rows_kernel, streamed),
        out_shape=jax.ShapeDtypeStruct((FRAMES * COUNT, C), jnp.float32),
        in_specs=[VMEM, VMEM, pl.BlockSpec(memory_space=pltpu.HBM) if streamed else VMEM],
        out_specs=VMEM,
        scratch_shapes=[
            pltpu.VMEM((FRAMES, ROWS + 2, WIDE + 8, C), jnp.float32),
            pltpu.VMEM((FRAMES * COUNT, 9 * C), jnp.bfloat16),
        ]
        + streamed * [pltpu.VMEM((3, 9 * C, C), jnp.bfloat16), pltpu.SemaphoreType.DMA((3, 4))],
        compiler_params=STREAM_PARAMS if streamed else CONV_PARAMS,
        cost_estimate=pl.CostEstimate(
            flops=2 * 768 * 27 * C * C, bytes_accessed=27 * C * C * 2, transcendentals=10**6
        ),
    )(main, gain, pltpu.with_memory_space_constraint(weight, pltpu.HBM) if streamed else weight)
    operands = [total, above, below, gain, weight, latent if add else first_column]
    scratch = [
        pltpu.VMEM((2, FRAMES, WIDE + 8, C), jnp.float32),
        pltpu.VMEM((2, FRAMES * WIDE, 3 * C), jnp.bfloat16),
        pltpu.VMEM((2, FRAMES * WIDE, C), jnp.float32),
    ]
    if add:
        scratch.append(pltpu.VMEM((ROWS, WIDE + 8, C), jnp.float32))
        scratch.append(pltpu.VMEM((POS, C), jnp.float32))
    return pl.pallas_call(
        functools.partial(edge_rows_kernel, add),
        out_shape=jax.ShapeDtypeStruct((FRAMES, POS if add else COUNT, C), jnp.bfloat16),
        in_specs=[VMEM] * 5 + [VMEM if add else pl.BlockSpec(memory_space=pltpu.SMEM)],
        out_specs=VMEM,
        scratch_shapes=scratch,
        compiler_params=CONV_PARAMS,
        cost_estimate=pl.CostEstimate(
            flops=2 * 384 * 9 * C * C, bytes_accessed=27 * C * C * 2, transcendentals=10**5
        ),
    )(*operands)


def attend_kernel(count, group, start, end, *refs):
    if start:
        rows_ref, query_weight_ref, key_weight_ref = refs[:3]
        refs = refs[3:]
        scale = math.log2(math.e) / math.sqrt(C)
        query = jnp.dot(
            rows_ref[...], query_weight_ref[...], preferred_element_type=jnp.float32
        ).astype(jnp.bfloat16)
        query = lax.dot_general(
            query, key_weight_ref[...], ROW_DOT, preferred_element_type=jnp.float32
        )
        query = (query * scale).astype(jnp.bfloat16)
        top = summed = acc = None
    else:
        query_ref, acc_in, top_in, sum_in = refs[:4]
        refs = refs[4:]
        query = query_ref[...]
        top, summed, acc = top_in[:, :1], sum_in[:, :1], acc_in[...]
    blocks, outs = refs[:count], refs[count:]
    parts = [
        block[first : first + TILE, :]
        for block in blocks
        for first in range(0, block.shape[0], TILE)
    ]
    keys = [
        parts[first] if group == 1 else jnp.concatenate(parts[first : first + group], 0)
        for first in range(0, len(parts), group)
    ]

    def score(key):
        return lax.dot_general(query, key, ROW_DOT, preferred_element_type=jnp.float32)

    following = score(keys[0])
    for index, key in enumerate(keys):
        scores = following
        if index + 1 < len(keys):
            following = score(keys[index + 1])
        ceiling = scores.max(-1, keepdims=True)
        if top is not None:
            ceiling = jnp.maximum(ceiling, top)
        weights = jnp.exp2(scores - ceiling)
        new_sum = weights.sum(-1, keepdims=True)
        new_acc = jnp.dot(weights.astype(jnp.bfloat16), key, preferred_element_type=jnp.float32)
        if top is not None:
            shrink = jnp.exp2(top - ceiling)
            new_sum = summed * shrink + new_sum
            new_acc = acc * shrink + new_acc
        top, summed, acc = ceiling, new_sum, new_acc
    if end:
        share_out, level_out = outs
        share_out[...] = (acc / summed).astype(jnp.bfloat16)
        level_out[...] = jnp.broadcast_to(top + jnp.log2(summed), level_out.shape)
        return
    if start:
        outs[0][...] = query
        outs = outs[1:]
    acc_out, top_out, sum_out = outs
    acc_out[...] = acc
    top_out[...] = jnp.broadcast_to(top, top_out.shape)
    sum_out[...] = jnp.broadcast_to(summed, sum_out.shape)


def attend(source, blocks, group=1, start=False, end=False):
    rows = source[0].shape[0]
    keys = sum(block.shape[0] for block in blocks)
    operands = [*source, *blocks]
    bf16 = jax.ShapeDtypeStruct((rows, C), jnp.bfloat16)
    column = jax.ShapeDtypeStruct((rows, 128), jnp.float32)
    outs = (jax.ShapeDtypeStruct((rows, C), jnp.float32), column, column)
    if end:
        outs = (bf16, column)
    elif start:
        outs = (bf16, *outs)
    return pl.pallas_call(
        functools.partial(attend_kernel, len(blocks), group, start, end),
        out_shape=outs,
        in_specs=[VMEM] * len(operands),
        out_specs=tuple(VMEM for _ in outs),
        compiler_params=PARAMS,
        cost_estimate=pl.CostEstimate(
            flops=4 * rows * keys * C, bytes_accessed=2 * keys * C, transcendentals=rows * keys
        ),
    )(*operands)


def finish_kernel(
    acc_ref, top_ref, sum_ref, other_ref, level_ref, state_ref, value_ref, outw_ref, out_ref, field
):
    own = top_ref[:, :1] + jnp.log2(sum_ref[:, :1])
    other = level_ref[...]
    ceiling = jnp.maximum(own, other)
    own_part = jnp.exp2(own - ceiling)
    other_part = jnp.exp2(other - ceiling)
    mixed = acc_ref[...] * (own_part / sum_ref[:, :1]) + other_ref[...].astype(jnp.float32) * (
        other_part
    )
    mixed = (mixed / (own_part + other_part)).astype(jnp.bfloat16)
    attended = jnp.dot(mixed, value_ref[...], preferred_element_type=jnp.float32)
    result = jnp.dot(
        attended.astype(jnp.bfloat16), outw_ref[...], preferred_element_type=jnp.float32
    ) + state_ref[...].astype(jnp.float32)
    for block in range(FRAMES):
        for row in range(ROWS):
            start = (block * ROWS + row) * OWN
            field[row, block * OWN : block * OWN + OWN, :] = result[start : start + OWN, :]
    out_ref[0] = field[...].astype(jnp.bfloat16)


def finish(state, other, level, flat, value_weight, out_weight):
    return pl.pallas_call(
        finish_kernel,
        out_shape=jax.ShapeDtypeStruct((1, ROWS, COLS, C), jnp.bfloat16),
        in_specs=[VMEM] * 8,
        out_specs=VMEM,
        scratch_shapes=[pltpu.VMEM((ROWS, COLS, C), jnp.float32)],
        compiler_params=PARAMS,
    )(*state, other, level, flat, value_weight, out_weight)


def row_halos(field, even, outermost):
    top, bottom = field[:, :WIDE, :], field[:, (ROWS - 1) * WIDE :, :]
    far = send(jnp.where(even, top, bottom), NEXT_CHIP)
    near = send(jnp.where(even, bottom, top), CORE)
    far = jnp.where(outermost, jnp.bfloat16(0), far)
    return jnp.where(even, far, near), jnp.where(even, near, far)


def body(
    latent,
    norm1_gain,
    conv1_weight,
    norm2_gain,
    conv2_weight,
    attn_gain,
    query_weight,
    key_weight,
    value_weight,
    out_weight,
):
    tile = lax.axis_index("tile")
    place = (
        tile % 2 == 0,
        (tile == 0) | (tile == 15),
        (OWN * lax.axis_index("frame") - 1).reshape(1),
    )
    latent, place = lax.optimization_barrier((latent, place))
    field, norm1_gain, norm2_gain = lax.optimization_barrier(
        (lax.all_to_all(pack(latent), "frame", 0, 0), norm1_gain, norm2_gain)
    )
    conv_one = convolve(field, place, norm1_gain, conv1_weight.reshape(3, 9 * C, C))
    hstate = convolve(
        conv_one, place, norm2_gain, conv2_weight.reshape(3, 9 * C, C), field
    )
    flat = lax.all_to_all(hstate, "frame", 0, 0).reshape(FRAMES * POS, C)
    flat, attn_gain, query_weight, key_weight, value_weight, out_weight = (
        lax.optimization_barrier(
            (flat, attn_gain, query_weight, key_weight, value_weight, out_weight)
        )
    )
    normed = norm_gain(flat.astype(jnp.float32), attn_gain).astype(jnp.bfloat16)
    half = TILE // 2
    low, high = normed[:half], normed[half:]
    behind_low = send(low, UP_X)
    ahead_high = send(high, DOWN_X)
    across = send(normed, OTHER_Z)
    mate = send(normed, CORE)
    normed, mate, low, high = lax.optimization_barrier((normed, mate, low, high))
    behind_high = send(high, UP_X)
    ahead_low = send(low, DOWN_X)
    own = attend([normed, query_weight, key_weight], [normed, mate], start=True)
    (behind_low, ahead_high, own) = lax.optimization_barrier((behind_low, ahead_high, own))
    far_low = send(behind_low, UP_X)
    far_high = send(ahead_high, DOWN_X)
    early = jnp.concatenate([behind_low, ahead_high], 0)
    late = jnp.concatenate([behind_high, ahead_low], 0)
    near_mate = send(jnp.concatenate([early, late], 0), CORE)
    other_query, *other = attend(
        [across, query_weight, key_weight], [mate, early, late], start=True
    )
    (far_low, far_high, other) = lax.optimization_barrier((far_low, far_high, other))
    far = jnp.concatenate([far_low, far_high], 0)
    far_mate = send(far, CORE)
    other = attend([other_query, *other], [near_mate])
    share, level = attend([other_query, *other], [far, far_mate], end=True)
    share_back = send(share, OTHER_Z)
    level_back = send(level[:, 0], OTHER_Z)
    own = lax.optimization_barrier((own, share))[0]
    own = attend(own, [across, early, late, near_mate, far, far_mate], group=2)
    return finish(own, share_back, level_back.reshape(-1, 1), flat, value_weight, out_weight)


def solution(mesh):
    return jax.shard_map(
        body,
        mesh=mesh,
        in_specs=(P("frame", "tile", None, None), P(), P(), P(), P(), P(), P(), P(), P(), P()),
        out_specs=P("frame", "tile", None, None),
        check_vma=False,
    )
```

```python
import functools
import math

import jax
import jax.numpy as jnp
from jax import lax
from jax.experimental import pallas as pl
from jax.experimental.pallas import tpu as pltpu
from jax.sharding import PartitionSpec as P

C = 384
FRAMES = 8
ROWS = 4
COLS = 160
OWN = COLS // FRAMES
WIDE = OWN + 4
POS = ROWS * OWN
TILE = FRAMES * POS
BOTH = ("frame", "tile")
VMEM = pl.BlockSpec(memory_space=pltpu.VMEM)
PARAMS = pltpu.CompilerParams(vmem_limit_bytes=24 * 2**20)
CONV_PARAMS = pltpu.CompilerParams(vmem_limit_bytes=28 * 2**20)
STREAM_PARAMS = pltpu.CompilerParams(vmem_limit_bytes=34 * 2**20)
ROW_DOT = (((1,), (1,)), ((), ()))


def coords(device):
    frame, tile = divmod(device, 16)
    return frame, tile // 4, tile // 2 % 2, tile % 2


def permutation(move):
    pairs = []
    for device in range(128):
        frame, x, z, core = move(*coords(device))
        pairs.append((device, frame * 16 + x % 4 * 4 + z % 2 * 2 + core % 2))
    return pairs


CORE = permutation(lambda f, x, z, c: (f, x, z, c + 1))
UP_X = permutation(lambda f, x, z, c: (f, x + 1, z, c))
DOWN_X = permutation(lambda f, x, z, c: (f, x - 1, z, c))
OTHER_Z = permutation(lambda f, x, z, c: (f, x, z + 1, c))

NEXT_CHIP = [
    (f * 16 + i, f * 16 + (i + (1 if i % 2 else 15)) % 16) for f in range(FRAMES) for i in range(16)
]


def send(value, pairs):
    return lax.ppermute(value, BOTH, pairs)


def norm_gain(field, gain):
    squares = jnp.mean(field * field, axis=-1, keepdims=True)
    return field * lax.rsqrt(squares + 1e-06) * gain.astype(jnp.float32)


def silu(u):
    return u / (1.0 + jnp.exp(-u))


def pack_kernel(latent_ref, out_ref, field):
    field[:, 0:8, :] = jnp.zeros((ROWS, 8, C), jnp.float32)
    field[:, COLS + 8 : COLS + 16, :] = jnp.zeros((ROWS, 8, C), jnp.float32)
    field[:, 8 : COLS + 8, :] = latent_ref[0].astype(jnp.float32)
    for block in range(FRAMES):
        start = 6 + OWN * block
        piece = field[:, start : start + WIDE, :]
        out_ref[block] = piece.reshape(ROWS * WIDE, C).astype(jnp.bfloat16)


def pack(latent):
    return pl.pallas_call(
        pack_kernel,
        out_shape=jax.ShapeDtypeStruct((FRAMES, ROWS * WIDE, C), jnp.bfloat16),
        in_specs=[VMEM],
        out_specs=VMEM,
        scratch_shapes=[pltpu.VMEM((ROWS, COLS + 16, C), jnp.float32)],
        compiler_params=PARAMS,
    )(latent)


COUNT = ROWS * WIDE


def activate(value, gain_ref):
    return silu(norm_gain(value, gain_ref[...].reshape(1, 1, C)))


def time_taps(weight_ref, taps, times):
    return jnp.concatenate([weight_ref[time, taps, :] for time in times], 1)


def own_rows_kernel(streamed, main_ref, gain_ref, weight_ref, total_ref, field, stacked, *refs):
    if streamed:
        source, (weight_ref, arrived) = weight_ref, refs
        copies = []
        for time in range(3):
            for part in range(4):
                rows = pl.ds(part * 864, 864)
                copies.append(
                    pltpu.make_async_copy(
                        source.at[time, rows], weight_ref.at[time, rows], arrived.at[time, part]
                    )
                )
        for copy in copies:
            copy.start()
    field[:, :, WIDE:, :] = jnp.zeros((FRAMES, ROWS + 2, 8, C), jnp.float32)
    field[:, 0:1, 0:WIDE, :] = jnp.zeros((FRAMES, 1, WIDE, C), jnp.float32)
    field[:, ROWS + 1 :, 0:WIDE, :] = jnp.zeros((FRAMES, 1, WIDE, C), jnp.float32)

    for t in range(FRAMES):
        main = main_ref[t].astype(jnp.float32).reshape(ROWS, WIDE, C)
        field[t, 1 : ROWS + 1, 0:WIDE, :] = activate(main, gain_ref)
        for dh in range(3):
            for dw in range(3):
                piece = field[t, dh : dh + ROWS, dw : dw + WIDE, :]
                lanes = (dh * 3 + dw) * C
                stacked[t * COUNT : t * COUNT + COUNT, lanes : lanes + C] = piece.reshape(
                    COUNT, C
                ).astype(jnp.bfloat16)
    if streamed:
        for copy in copies[:4]:
            copy.wait()
        total_ref[: 2 * COUNT, :] = jnp.zeros((2 * COUNT, C), jnp.float32)
        total_ref[2 * COUNT :, :] = jnp.dot(
            stacked[: 6 * COUNT, :],
            time_taps(weight_ref, slice(0, 9 * C), (0,)),
            preferred_element_type=jnp.float32,
        )
        for copy in copies[4:]:
            copy.wait()
    pair = time_taps(weight_ref, slice(0, 9 * C), (2, 1))
    both = jnp.dot(stacked[...], pair, preferred_element_type=jnp.float32)
    if streamed:
        total_ref[...] += both[:, :C]
    else:
        total_ref[...] = both[:, :C]
    total_ref[COUNT:, :] += both[: 7 * COUNT, C:]
    if not streamed:
        total_ref[2 * COUNT :, :] += jnp.dot(
            stacked[: 6 * COUNT, :],
            time_taps(weight_ref, slice(0, 9 * C), (0,)),
            preferred_element_type=jnp.float32,
        )


def edge_rows_kernel(add, total_ref, above_ref, below_ref, gain_ref, weight_ref, *refs):
    if add:
        latent_ref, out_ref, field, stacked, edge, shifted, trimmed = refs
    else:
        first_ref, out_ref, field, stacked, edge = refs
        column = lax.broadcasted_iota(jnp.int32, (ROWS, WIDE, C), 1).reshape(COUNT, C)
        column = column + first_ref[0]
        inside = (column >= 0) & (column < COLS)
    for side, rows_ref in enumerate((above_ref, below_ref)):
        field[side, :, WIDE:, :] = jnp.zeros((FRAMES, 8, C), jnp.float32)
        field[side, :, 0:WIDE, :] = activate(rows_ref[...].astype(jnp.float32), gain_ref)
        for dw in range(3):
            piece = field[side, :, dw : dw + WIDE, :]
            stacked[side, :, dw * C : dw * C + C] = piece.reshape(FRAMES * WIDE, C).astype(
                jnp.bfloat16
            )
        taps = slice(side * 6 * C, side * 6 * C + 3 * C)
        weights = time_taps(weight_ref, taps, (2, 1, 0))
        three = jnp.dot(stacked[side], weights, preferred_element_type=jnp.float32)
        edge[side] = three[:, :C]
        edge[side, WIDE:, :] += three[: 7 * WIDE, C : 2 * C]
        edge[side, 2 * WIDE :, :] += three[: 6 * WIDE, 2 * C :]
    for t in range(FRAMES):
        value = total_ref[t * COUNT : t * COUNT + COUNT, :]
        rows = slice(t * WIDE, t * WIDE + WIDE)
        value = jnp.concatenate(
            [
                value[:WIDE] + edge[0, rows, :],
                value[WIDE : 3 * WIDE],
                value[3 * WIDE :] + edge[1, rows, :],
            ],
            0,
        )
        if not add:
            out_ref[t] = jnp.where(inside, value, 0.0).astype(jnp.bfloat16)
            continue
        shifted[:, 8 : WIDE + 8, :] = latent_ref[t].astype(jnp.float32).reshape(ROWS, WIDE, C)
        value = value.reshape(ROWS, WIDE, C)[:, :OWN, :] + shifted[:, 10 : OWN + 10, :]
        for row in range(ROWS):
            trimmed[row * OWN : row * OWN + OWN, :] = value[row]
        out_ref[t] = trimmed[...].astype(jnp.bfloat16)


def convolve(main, place, gain, weight, latent=None):
    add = latent is not None
    gain = gain.reshape(1, C)
    even, outermost, first_column = place
    above, below = row_halos(main, even, outermost)
    streamed = not add
    total = pl.pallas_call(
        functools.partial(own_rows_kernel, streamed),
        out_shape=jax.ShapeDtypeStruct((FRAMES * COUNT, C), jnp.float32),
        in_specs=[VMEM, VMEM, pl.BlockSpec(memory_space=pltpu.HBM) if streamed else VMEM],
        out_specs=VMEM,
        scratch_shapes=[
            pltpu.VMEM((FRAMES, ROWS + 2, WIDE + 8, C), jnp.float32),
            pltpu.VMEM((FRAMES * COUNT, 9 * C), jnp.bfloat16),
        ]
        + streamed * [pltpu.VMEM((3, 9 * C, C), jnp.bfloat16), pltpu.SemaphoreType.DMA((3, 4))],
        compiler_params=STREAM_PARAMS if streamed else CONV_PARAMS,
        cost_estimate=pl.CostEstimate(
            flops=2 * 768 * 27 * C * C, bytes_accessed=27 * C * C * 2, transcendentals=10**6
        ),
    )(main, gain, pltpu.with_memory_space_constraint(weight, pltpu.HBM) if streamed else weight)
    operands = [total, above, below, gain, weight, latent if add else first_column]
    scratch = [
        pltpu.VMEM((2, FRAMES, WIDE + 8, C), jnp.float32),
        pltpu.VMEM((2, FRAMES * WIDE, 3 * C), jnp.bfloat16),
        pltpu.VMEM((2, FRAMES * WIDE, C), jnp.float32),
    ]
    if add:
        scratch.append(pltpu.VMEM((ROWS, WIDE + 8, C), jnp.float32))
        scratch.append(pltpu.VMEM((POS, C), jnp.float32))
    return pl.pallas_call(
        functools.partial(edge_rows_kernel, add),
        out_shape=jax.ShapeDtypeStruct((FRAMES, POS if add else COUNT, C), jnp.bfloat16),
        in_specs=[VMEM] * 5 + [VMEM if add else pl.BlockSpec(memory_space=pltpu.SMEM)],
        out_specs=VMEM,
        scratch_shapes=scratch,
        compiler_params=CONV_PARAMS,
        cost_estimate=pl.CostEstimate(
            flops=2 * 384 * 9 * C * C, bytes_accessed=27 * C * C * 2, transcendentals=10**5
        ),
    )(*operands)


def attend_kernel(count, group, start, end, *refs):
    if start:
        rows_ref, query_weight_ref, key_weight_ref = refs[:3]
        refs = refs[3:]
        scale = math.log2(math.e) / math.sqrt(C)
        query = jnp.dot(
            rows_ref[...], query_weight_ref[...], preferred_element_type=jnp.float32
        ).astype(jnp.bfloat16)
        query = lax.dot_general(
            query, key_weight_ref[...], ROW_DOT, preferred_element_type=jnp.float32
        )
        query = (query * scale).astype(jnp.bfloat16)
        top = summed = acc = None
    else:
        query_ref, acc_in, top_in, sum_in = refs[:4]
        refs = refs[4:]
        query = query_ref[...]
        top, summed, acc = top_in[:, :1], sum_in[:, :1], acc_in[...]
    blocks, outs = refs[:count], refs[count:]
    parts = [
        block[first : first + TILE, :]
        for block in blocks
        for first in range(0, block.shape[0], TILE)
    ]
    keys = [
        parts[first] if group == 1 else jnp.concatenate(parts[first : first + group], 0)
        for first in range(0, len(parts), group)
    ]

    def score(key):
        return lax.dot_general(query, key, ROW_DOT, preferred_element_type=jnp.float32)

    following = score(keys[0])
    for index, key in enumerate(keys):
        scores = following
        if index + 1 < len(keys):
            following = score(keys[index + 1])
        ceiling = scores.max(-1, keepdims=True)
        if top is not None:
            ceiling = jnp.maximum(ceiling, top)
        weights = jnp.exp2(scores - ceiling)
        new_sum = weights.sum(-1, keepdims=True)
        new_acc = jnp.dot(weights.astype(jnp.bfloat16), key, preferred_element_type=jnp.float32)
        if top is not None:
            shrink = jnp.exp2(top - ceiling)
            new_sum = summed * shrink + new_sum
            new_acc = acc * shrink + new_acc
        top, summed, acc = ceiling, new_sum, new_acc
    if end:
        share_out, level_out = outs
        share_out[...] = (acc / summed).astype(jnp.bfloat16)
        level_out[...] = jnp.broadcast_to(top + jnp.log2(summed), level_out.shape)
        return
    if start:
        outs[0][...] = query
        outs = outs[1:]
    acc_out, top_out, sum_out = outs
    acc_out[...] = acc
    top_out[...] = jnp.broadcast_to(top, top_out.shape)
    sum_out[...] = jnp.broadcast_to(summed, sum_out.shape)


def attend(source, blocks, group=1, start=False, end=False):
    rows = source[0].shape[0]
    keys = sum(block.shape[0] for block in blocks)
    operands = [*source, *blocks]
    bf16 = jax.ShapeDtypeStruct((rows, C), jnp.bfloat16)
    column = jax.ShapeDtypeStruct((rows, 128), jnp.float32)
    outs = (jax.ShapeDtypeStruct((rows, C), jnp.float32), column, column)
    if end:
        outs = (bf16, column)
    elif start:
        outs = (bf16, *outs)
    return pl.pallas_call(
        functools.partial(attend_kernel, len(blocks), group, start, end),
        out_shape=outs,
        in_specs=[VMEM] * len(operands),
        out_specs=tuple(VMEM for _ in outs),
        compiler_params=PARAMS,
        cost_estimate=pl.CostEstimate(
            flops=4 * rows * keys * C, bytes_accessed=2 * keys * C, transcendentals=rows * keys
        ),
    )(*operands)


def finish_kernel(
    acc_ref, top_ref, sum_ref, other_ref, level_ref, state_ref, value_ref, outw_ref, out_ref, field
):
    own = top_ref[:, :1] + jnp.log2(sum_ref[:, :1])
    other = level_ref[...]
    ceiling = jnp.maximum(own, other)
    own_part = jnp.exp2(own - ceiling)
    other_part = jnp.exp2(other - ceiling)
    mixed = acc_ref[...] * (own_part / sum_ref[:, :1]) + other_ref[...].astype(jnp.float32) * (
        other_part
    )
    mixed = (mixed / (own_part + other_part)).astype(jnp.bfloat16)
    attended = jnp.dot(mixed, value_ref[...], preferred_element_type=jnp.float32)
    result = jnp.dot(
        attended.astype(jnp.bfloat16), outw_ref[...], preferred_element_type=jnp.float32
    ) + state_ref[...].astype(jnp.float32)
    for block in range(FRAMES):
        for row in range(ROWS):
            start = (block * ROWS + row) * OWN
            field[row, block * OWN : block * OWN + OWN, :] = result[start : start + OWN, :]
    out_ref[0] = field[...].astype(jnp.bfloat16)


def finish(state, other, level, flat, value_weight, out_weight):
    return pl.pallas_call(
        finish_kernel,
        out_shape=jax.ShapeDtypeStruct((1, ROWS, COLS, C), jnp.bfloat16),
        in_specs=[VMEM] * 8,
        out_specs=VMEM,
        scratch_shapes=[pltpu.VMEM((ROWS, COLS, C), jnp.float32)],
        compiler_params=PARAMS,
    )(*state, other, level, flat, value_weight, out_weight)


def row_halos(field, even, outermost):
    top, bottom = field[:, :WIDE, :], field[:, (ROWS - 1) * WIDE :, :]
    far = send(jnp.where(even, top, bottom), NEXT_CHIP)
    near = send(jnp.where(even, bottom, top), CORE)
    far = jnp.where(outermost, jnp.bfloat16(0), far)
    return jnp.where(even, far, near), jnp.where(even, near, far)


def body(
    latent,
    norm1_gain,
    conv1_weight,
    norm2_gain,
    conv2_weight,
    attn_gain,
    query_weight,
    key_weight,
    value_weight,
    out_weight,
):
    tile = lax.axis_index("tile")
    place = (
        tile % 2 == 0,
        (tile == 0) | (tile == 15),
        (OWN * lax.axis_index("frame") - 1).reshape(1),
    )
    latent, place = lax.optimization_barrier((latent, place))
    field, norm1_gain, norm2_gain = lax.optimization_barrier(
        (lax.all_to_all(pack(latent), "frame", 0, 0), norm1_gain, norm2_gain)
    )
    conv_one = convolve(field, place, norm1_gain, conv1_weight.reshape(3, 9 * C, C))
    hstate = convolve(
        conv_one, place, norm2_gain, conv2_weight.reshape(3, 9 * C, C), field
    )
    flat = lax.all_to_all(hstate, "frame", 0, 0).reshape(FRAMES * POS, C)
    flat, attn_gain, query_weight, key_weight, value_weight, out_weight = (
        lax.optimization_barrier(
            (flat, attn_gain, query_weight, key_weight, value_weight, out_weight)
        )
    )
    normed = norm_gain(flat.astype(jnp.float32), attn_gain).astype(jnp.bfloat16)
    half = TILE // 2
    low, high = normed[:half], normed[half:]
    behind_low = send(low, UP_X)
    ahead_high = send(high, DOWN_X)
    across = send(normed, OTHER_Z)
    mate = send(normed, CORE)
    normed, mate, low, high = lax.optimization_barrier((normed, mate, low, high))
    behind_high = send(high, UP_X)
    ahead_low = send(low, DOWN_X)
    own = attend([normed, query_weight, key_weight], [normed, mate], start=True)
    (behind_low, ahead_high, own) = lax.optimization_barrier((behind_low, ahead_high, own))
    far_low = send(behind_low, UP_X)
    far_high = send(ahead_high, DOWN_X)
    early = jnp.concatenate([behind_low, ahead_high], 0)
    late = jnp.concatenate([behind_high, ahead_low], 0)
    near_mate = send(jnp.concatenate([early, late], 0), CORE)
    other_query, *other = attend(
        [across, query_weight, key_weight], [mate, early, late], start=True
    )
    (far_low, far_high, other) = lax.optimization_barrier((far_low, far_high, other))
    far = jnp.concatenate([far_low, far_high], 0)
    far_mate = send(far, CORE)
    other = attend([other_query, *other], [near_mate])
    share, level = attend([other_query, *other], [far, far_mate], end=True)
    share_back = send(share, OTHER_Z)
    level_back = send(level[:, 0], OTHER_Z)
    own = lax.optimization_barrier((own, share))[0]
    own = attend(own, [across, early, late, near_mate, far, far_mate], group=2)
    return finish(own, share_back, level_back.reshape(-1, 1), flat, value_weight, out_weight)


def solution(mesh):
    return jax.shard_map(
        body,
        mesh=mesh,
        in_specs=(P("frame", "tile", None, None), P(), P(), P(), P(), P(), P(), P(), P(), P()),
        out_specs=P("frame", "tile", None, None),
        check_vma=False,
    )
```

```python
import functools
import math

import jax
import jax.numpy as jnp
from jax import lax
from jax.experimental import pallas as pl
from jax.experimental.pallas import tpu as pltpu
from jax.sharding import PartitionSpec as P

C = 384
FRAMES = 8
ROWS = 4
COLS = 160
OWN = COLS // FRAMES
WIDE = OWN + 4
POS = ROWS * OWN
TILE = FRAMES * POS
BOTH = ("frame", "tile")
VMEM = pl.BlockSpec(memory_space=pltpu.VMEM)
PARAMS = pltpu.CompilerParams(vmem_limit_bytes=24 * 2**20)
FINISH_PARAMS = pltpu.CompilerParams(vmem_limit_bytes=48 * 2**20)
CONV_PARAMS = pltpu.CompilerParams(vmem_limit_bytes=28 * 2**20)
STREAM_PARAMS = pltpu.CompilerParams(vmem_limit_bytes=34 * 2**20)
ROW_DOT = (((1,), (1,)), ((), ()))


def coords(device):
    frame, tile = divmod(device, 16)
    return frame, tile // 4, tile // 2 % 2, tile % 2


def permutation(move):
    pairs = []
    for device in range(128):
        frame, x, z, core = move(*coords(device))
        pairs.append((device, frame * 16 + x % 4 * 4 + z % 2 * 2 + core % 2))
    return pairs


CORE = permutation(lambda f, x, z, c: (f, x, z, c + 1))
UP_X = permutation(lambda f, x, z, c: (f, x + 1, z, c))
DOWN_X = permutation(lambda f, x, z, c: (f, x - 1, z, c))
OTHER_Z = permutation(lambda f, x, z, c: (f, x, z + 1, c))

NEXT_CHIP = [
    (f * 16 + i, f * 16 + (i + (1 if i % 2 else 15)) % 16) for f in range(FRAMES) for i in range(16)
]


def send(value, pairs):
    return lax.ppermute(value, BOTH, pairs)


def norm_gain(field, gain):
    squares = jnp.mean(field * field, axis=-1, keepdims=True)
    return field * lax.rsqrt(squares + 1e-06) * gain.astype(jnp.float32)


def silu(u):
    return u / (1.0 + jnp.exp(-u))


def pack_kernel(latent_ref, out_ref, field):
    field[:, 0:8, :] = jnp.zeros((ROWS, 8, C), jnp.float32)
    field[:, COLS + 8 : COLS + 16, :] = jnp.zeros((ROWS, 8, C), jnp.float32)
    field[:, 8 : COLS + 8, :] = latent_ref[0].astype(jnp.float32)
    for block in range(FRAMES):
        start = 6 + OWN * block
        piece = field[:, start : start + WIDE, :]
        out_ref[block] = piece.reshape(ROWS * WIDE, C).astype(jnp.bfloat16)


def pack(latent):
    return pl.pallas_call(
        pack_kernel,
        out_shape=jax.ShapeDtypeStruct((FRAMES, ROWS * WIDE, C), jnp.bfloat16),
        in_specs=[VMEM],
        out_specs=VMEM,
        scratch_shapes=[pltpu.VMEM((ROWS, COLS + 16, C), jnp.float32)],
        compiler_params=PARAMS,
    )(latent)


COUNT = ROWS * WIDE


def activate(value, gain_ref):
    return silu(norm_gain(value, gain_ref[...].reshape(1, 1, C)))


def time_taps(weight_ref, taps, times):
    return jnp.concatenate([weight_ref[time, taps, :] for time in times], 1)


def own_rows_kernel(streamed, main_ref, gain_ref, weight_ref, total_ref, field, stacked, *refs):
    if streamed:
        source, (weight_ref, arrived) = weight_ref, refs
        copies = []
        for time in range(3):
            for part in range(4):
                rows = pl.ds(part * 864, 864)
                copies.append(
                    pltpu.make_async_copy(
                        source.at[time, rows], weight_ref.at[time, rows], arrived.at[time, part]
                    )
                )
        for copy in copies:
            copy.start()
    field[:, :, WIDE:, :] = jnp.zeros((FRAMES, ROWS + 2, 8, C), jnp.float32)
    field[:, 0:1, 0:WIDE, :] = jnp.zeros((FRAMES, 1, WIDE, C), jnp.float32)
    field[:, ROWS + 1 :, 0:WIDE, :] = jnp.zeros((FRAMES, 1, WIDE, C), jnp.float32)

    for t in range(FRAMES):
        main = main_ref[t].astype(jnp.float32).reshape(ROWS, WIDE, C)
        field[t, 1 : ROWS + 1, 0:WIDE, :] = activate(main, gain_ref)
        for dh in range(3):
            for dw in range(3):
                piece = field[t, dh : dh + ROWS, dw : dw + WIDE, :]
                lanes = (dh * 3 + dw) * C
                stacked[t * COUNT : t * COUNT + COUNT, lanes : lanes + C] = piece.reshape(
                    COUNT, C
                ).astype(jnp.bfloat16)
    if streamed:
        for copy in copies[:4]:
            copy.wait()
        total_ref[: 2 * COUNT, :] = jnp.zeros((2 * COUNT, C), jnp.float32)
        total_ref[2 * COUNT :, :] = jnp.dot(
            stacked[: 6 * COUNT, :],
            time_taps(weight_ref, slice(0, 9 * C), (0,)),
            preferred_element_type=jnp.float32,
        )
        for copy in copies[4:]:
            copy.wait()
    pair = time_taps(weight_ref, slice(0, 9 * C), (2, 1))
    both = jnp.dot(stacked[...], pair, preferred_element_type=jnp.float32)
    if streamed:
        total_ref[...] += both[:, :C]
    else:
        total_ref[...] = both[:, :C]
    total_ref[COUNT:, :] += both[: 7 * COUNT, C:]
    if not streamed:
        total_ref[2 * COUNT :, :] += jnp.dot(
            stacked[: 6 * COUNT, :],
            time_taps(weight_ref, slice(0, 9 * C), (0,)),
            preferred_element_type=jnp.float32,
        )


def edge_rows_kernel(add, total_ref, above_ref, below_ref, gain_ref, weight_ref, *refs):
    if add:
        latent_ref, out_ref, field, stacked, edge, shifted, trimmed = refs
    else:
        first_ref, out_ref, field, stacked, edge = refs
        column = lax.broadcasted_iota(jnp.int32, (ROWS, WIDE, C), 1).reshape(COUNT, C)
        column = column + first_ref[0]
        inside = (column >= 0) & (column < COLS)
    for side, rows_ref in enumerate((above_ref, below_ref)):
        field[side, :, WIDE:, :] = jnp.zeros((FRAMES, 8, C), jnp.float32)
        field[side, :, 0:WIDE, :] = activate(rows_ref[...].astype(jnp.float32), gain_ref)
        for dw in range(3):
            piece = field[side, :, dw : dw + WIDE, :]
            stacked[side, :, dw * C : dw * C + C] = piece.reshape(FRAMES * WIDE, C).astype(
                jnp.bfloat16
            )
        taps = slice(side * 6 * C, side * 6 * C + 3 * C)
        weights = time_taps(weight_ref, taps, (2, 1, 0))
        three = jnp.dot(stacked[side], weights, preferred_element_type=jnp.float32)
        edge[side] = three[:, :C]
        edge[side, WIDE:, :] += three[: 7 * WIDE, C : 2 * C]
        edge[side, 2 * WIDE :, :] += three[: 6 * WIDE, 2 * C :]
    for t in range(FRAMES):
        value = total_ref[t * COUNT : t * COUNT + COUNT, :]
        rows = slice(t * WIDE, t * WIDE + WIDE)
        value = jnp.concatenate(
            [
                value[:WIDE] + edge[0, rows, :],
                value[WIDE : 3 * WIDE],
                value[3 * WIDE :] + edge[1, rows, :],
            ],
            0,
        )
        if not add:
            out_ref[t] = jnp.where(inside, value, 0.0).astype(jnp.bfloat16)
            continue
        shifted[:, 8 : WIDE + 8, :] = latent_ref[t].astype(jnp.float32).reshape(ROWS, WIDE, C)
        value = value.reshape(ROWS, WIDE, C)[:, :OWN, :] + shifted[:, 10 : OWN + 10, :]
        for row in range(ROWS):
            trimmed[row * OWN : row * OWN + OWN, :] = value[row]
        out_ref[t] = trimmed[...].astype(jnp.bfloat16)


def convolve(main, place, gain, weight, latent=None):
    add = latent is not None
    gain = gain.reshape(1, C)
    even, outermost, first_column = place
    above, below = row_halos(main, even, outermost)
    streamed = not add
    total = pl.pallas_call(
        functools.partial(own_rows_kernel, streamed),
        out_shape=jax.ShapeDtypeStruct((FRAMES * COUNT, C), jnp.float32),
        in_specs=[VMEM, VMEM, pl.BlockSpec(memory_space=pltpu.HBM) if streamed else VMEM],
        out_specs=VMEM,
        scratch_shapes=[
            pltpu.VMEM((FRAMES, ROWS + 2, WIDE + 8, C), jnp.float32),
            pltpu.VMEM((FRAMES * COUNT, 9 * C), jnp.bfloat16),
        ]
        + streamed * [pltpu.VMEM((3, 9 * C, C), jnp.bfloat16), pltpu.SemaphoreType.DMA((3, 4))],
        compiler_params=STREAM_PARAMS if streamed else CONV_PARAMS,
        cost_estimate=pl.CostEstimate(
            flops=2 * 768 * 27 * C * C, bytes_accessed=27 * C * C * 2, transcendentals=10**6
        ),
    )(main, gain, pltpu.with_memory_space_constraint(weight, pltpu.HBM) if streamed else weight)
    operands = [total, above, below, gain, weight, latent if add else first_column]
    scratch = [
        pltpu.VMEM((2, FRAMES, WIDE + 8, C), jnp.float32),
        pltpu.VMEM((2, FRAMES * WIDE, 3 * C), jnp.bfloat16),
        pltpu.VMEM((2, FRAMES * WIDE, C), jnp.float32),
    ]
    if add:
        scratch.append(pltpu.VMEM((ROWS, WIDE + 8, C), jnp.float32))
        scratch.append(pltpu.VMEM((POS, C), jnp.float32))
    return pl.pallas_call(
        functools.partial(edge_rows_kernel, add),
        out_shape=jax.ShapeDtypeStruct((FRAMES, POS if add else COUNT, C), jnp.bfloat16),
        in_specs=[VMEM] * 5 + [VMEM if add else pl.BlockSpec(memory_space=pltpu.SMEM)],
        out_specs=VMEM,
        scratch_shapes=scratch,
        compiler_params=CONV_PARAMS,
        cost_estimate=pl.CostEstimate(
            flops=2 * 384 * 9 * C * C, bytes_accessed=27 * C * C * 2, transcendentals=10**5
        ),
    )(*operands)


def attend_kernel(count, group, start, end, *refs):
    if start:
        rows_ref, query_weight_ref, key_weight_ref = refs[:3]
        refs = refs[3:]
        scale = math.log2(math.e) / math.sqrt(C)
        query = jnp.dot(
            rows_ref[...], query_weight_ref[...], preferred_element_type=jnp.float32
        ).astype(jnp.bfloat16)
        query = lax.dot_general(
            query, key_weight_ref[...], ROW_DOT, preferred_element_type=jnp.float32
        )
        query = (query * scale).astype(jnp.bfloat16)
        top = summed = acc = None
    else:
        query_ref, acc_in, top_in, sum_in = refs[:4]
        refs = refs[4:]
        query = query_ref[...]
        top, summed, acc = top_in[:, :1], sum_in[:, :1], acc_in[...]
    blocks, outs = refs[:count], refs[count:]
    parts = [
        block[first : first + TILE, :]
        for block in blocks
        for first in range(0, block.shape[0], TILE)
    ]
    keys = [
        parts[first] if group == 1 else jnp.concatenate(parts[first : first + group], 0)
        for first in range(0, len(parts), group)
    ]

    def score(key):
        return lax.dot_general(query, key, ROW_DOT, preferred_element_type=jnp.float32)

    following = score(keys[0])
    for index, key in enumerate(keys):
        scores = following
        if index + 1 < len(keys):
            following = score(keys[index + 1])
        ceiling = scores.max(-1, keepdims=True)
        if top is not None:
            ceiling = jnp.maximum(ceiling, top)
        weights = jnp.exp2(scores - ceiling)
        new_sum = weights.sum(-1, keepdims=True)
        new_acc = jnp.dot(weights.astype(jnp.bfloat16), key, preferred_element_type=jnp.float32)
        if top is not None:
            shrink = jnp.exp2(top - ceiling)
            new_sum = summed * shrink + new_sum
            new_acc = acc * shrink + new_acc
        top, summed, acc = ceiling, new_sum, new_acc
    if end:
        share_out, level_out = outs
        share_out[...] = (acc / summed).astype(jnp.bfloat16)
        level_out[...] = jnp.broadcast_to(top + jnp.log2(summed), level_out.shape)
        return
    if start:
        outs[0][...] = query
        outs = outs[1:]
    acc_out, top_out, sum_out = outs
    acc_out[...] = acc
    top_out[...] = jnp.broadcast_to(top, top_out.shape)
    sum_out[...] = jnp.broadcast_to(summed, sum_out.shape)


def attend(source, blocks, group=1, start=False, end=False):
    rows = source[0].shape[0]
    keys = sum(block.shape[0] for block in blocks)
    operands = [*source, *blocks]
    bf16 = jax.ShapeDtypeStruct((rows, C), jnp.bfloat16)
    column = jax.ShapeDtypeStruct((rows, 128), jnp.float32)
    outs = (jax.ShapeDtypeStruct((rows, C), jnp.float32), column, column)
    if end:
        outs = (bf16, column)
    elif start:
        outs = (bf16, *outs)
    return pl.pallas_call(
        functools.partial(attend_kernel, len(blocks), group, start, end),
        out_shape=outs,
        in_specs=[VMEM] * len(operands),
        out_specs=tuple(VMEM for _ in outs),
        compiler_params=PARAMS,
        cost_estimate=pl.CostEstimate(
            flops=4 * rows * keys * C, bytes_accessed=2 * keys * C, transcendentals=rows * keys
        ),
    )(*operands)


def finish_kernel(
    acc_ref, top_ref, sum_ref, other_ref, level_ref, state_ref, value_ref, outw_ref, out_ref, field
):
    own = top_ref[:, :1] + jnp.log2(sum_ref[:, :1])
    other = level_ref[...]
    ceiling = jnp.maximum(own, other)
    own_part = jnp.exp2(own - ceiling)
    other_part = jnp.exp2(other - ceiling)
    mixed = acc_ref[...] * (own_part / sum_ref[:, :1]) + other_ref[...].astype(jnp.float32) * (
        other_part
    )
    mixed = (mixed / (own_part + other_part)).astype(jnp.bfloat16)
    attended = jnp.dot(mixed, value_ref[...], preferred_element_type=jnp.float32)
    result = jnp.dot(
        attended.astype(jnp.bfloat16), outw_ref[...], preferred_element_type=jnp.float32
    ) + state_ref[...].astype(jnp.float32)
    for block in range(FRAMES):
        for row in range(ROWS):
            start = (block * ROWS + row) * OWN
            field[row, block * OWN : block * OWN + OWN, :] = result[start : start + OWN, :]
    out_ref[0] = field[...].astype(jnp.bfloat16)


def finish(state, other, level, flat, value_weight, out_weight):
    return pl.pallas_call(
        finish_kernel,
        out_shape=jax.ShapeDtypeStruct((1, ROWS, COLS, C), jnp.bfloat16),
        in_specs=[VMEM] * 8,
        out_specs=VMEM,
        scratch_shapes=[pltpu.VMEM((ROWS, COLS, C), jnp.float32)],
        compiler_params=FINISH_PARAMS,
    )(*state, other, level, flat, value_weight, out_weight)


def row_halos(field, even, outermost):
    top, bottom = field[:, :WIDE, :], field[:, (ROWS - 1) * WIDE :, :]
    far = send(jnp.where(even, top, bottom), NEXT_CHIP)
    near = send(jnp.where(even, bottom, top), CORE)
    far = jnp.where(outermost, jnp.bfloat16(0), far)
    return jnp.where(even, far, near), jnp.where(even, near, far)


def body(
    latent,
    norm1_gain,
    conv1_weight,
    norm2_gain,
    conv2_weight,
    attn_gain,
    query_weight,
    key_weight,
    value_weight,
    out_weight,
):
    tile = lax.axis_index("tile")
    place = (
        tile % 2 == 0,
        (tile == 0) | (tile == 15),
        (OWN * lax.axis_index("frame") - 1).reshape(1),
    )
    latent, place = lax.optimization_barrier((latent, place))
    field, norm1_gain, norm2_gain = lax.optimization_barrier(
        (lax.all_to_all(pack(latent), "frame", 0, 0), norm1_gain, norm2_gain)
    )
    conv_one = convolve(field, place, norm1_gain, conv1_weight.reshape(3, 9 * C, C))
    hstate = convolve(
        conv_one, place, norm2_gain, conv2_weight.reshape(3, 9 * C, C), field
    )
    flat = lax.all_to_all(hstate, "frame", 0, 0).reshape(FRAMES * POS, C)
    flat, attn_gain, query_weight, key_weight, value_weight, out_weight = (
        lax.optimization_barrier(
            (flat, attn_gain, query_weight, key_weight, value_weight, out_weight)
        )
    )
    normed = norm_gain(flat.astype(jnp.float32), attn_gain).astype(jnp.bfloat16)
    half = TILE // 2
    low, high = normed[:half], normed[half:]
    behind_low = send(low, UP_X)
    ahead_high = send(high, DOWN_X)
    across = send(normed, OTHER_Z)
    mate = send(normed, CORE)
    normed, mate, low, high = lax.optimization_barrier((normed, mate, low, high))
    behind_high = send(high, UP_X)
    ahead_low = send(low, DOWN_X)
    own = attend([normed, query_weight, key_weight], [normed, mate], start=True)
    (behind_low, ahead_high, own) = lax.optimization_barrier((behind_low, ahead_high, own))
    far_low = send(behind_low, UP_X)
    far_high = send(ahead_high, DOWN_X)
    early = jnp.concatenate([behind_low, ahead_high], 0)
    late = jnp.concatenate([behind_high, ahead_low], 0)
    near_mate = send(jnp.concatenate([early, late], 0), CORE)
    other_query, *other = attend(
        [across, query_weight, key_weight], [mate, early, late], start=True
    )
    (far_low, far_high, other) = lax.optimization_barrier((far_low, far_high, other))
    far = jnp.concatenate([far_low, far_high], 0)
    far_mate = send(far, CORE)
    other = attend([other_query, *other], [near_mate])
    share, level = attend([other_query, *other], [far, far_mate], end=True)
    share_back = send(share, OTHER_Z)
    level_back = send(level[:, 0], OTHER_Z)
    own = lax.optimization_barrier((own, share))[0]
    own = attend(own, [across, early, late, near_mate, far, far_mate], group=2)
    return finish(own, share_back, level_back.reshape(-1, 1), flat, value_weight, out_weight)


def solution(mesh):
    return jax.shard_map(
        body,
        mesh=mesh,
        in_specs=(P("frame", "tile", None, None), P(), P(), P(), P(), P(), P(), P(), P(), P()),
        out_specs=P("frame", "tile", None, None),
        check_vma=False,
    )
```

```python
import functools
import math

import jax
import jax.numpy as jnp
from jax import lax
from jax.experimental import pallas as pl
from jax.experimental.pallas import tpu as pltpu
from jax.sharding import PartitionSpec as P

C = 384
FRAMES = 8
ROWS = 4
COLS = 160
OWN = COLS // FRAMES
WIDE = OWN + 4
POS = ROWS * OWN
TILE = FRAMES * POS
BOTH = ("frame", "tile")
VMEM = pl.BlockSpec(memory_space=pltpu.VMEM)
PARAMS = pltpu.CompilerParams(vmem_limit_bytes=24 * 2**20)
CONV_PARAMS = pltpu.CompilerParams(vmem_limit_bytes=28 * 2**20)
STREAM_PARAMS = pltpu.CompilerParams(vmem_limit_bytes=34 * 2**20)
ROW_DOT = (((1,), (1,)), ((), ()))


def coords(device):
    frame, tile = divmod(device, 16)
    return frame, tile // 4, tile // 2 % 2, tile % 2


def permutation(move):
    pairs = []
    for device in range(128):
        frame, x, z, core = move(*coords(device))
        pairs.append((device, frame * 16 + x % 4 * 4 + z % 2 * 2 + core % 2))
    return pairs


CORE = permutation(lambda f, x, z, c: (f, x, z, c + 1))
UP_X = permutation(lambda f, x, z, c: (f, x + 1, z, c))
DOWN_X = permutation(lambda f, x, z, c: (f, x - 1, z, c))
OTHER_Z = permutation(lambda f, x, z, c: (f, x, z + 1, c))

NEXT_CHIP = [
    (f * 16 + i, f * 16 + (i + (1 if i % 2 else 15)) % 16) for f in range(FRAMES) for i in range(16)
]


def send(value, pairs):
    return lax.ppermute(value, BOTH, pairs)


def norm_gain(field, gain):
    squares = jnp.mean(field * field, axis=-1, keepdims=True)
    return field * lax.rsqrt(squares + 1e-06) * gain.astype(jnp.float32)


def silu(u):
    return u / (1.0 + jnp.exp(-u))


def pack_kernel(latent_ref, out_ref, field):
    field[:, 0:8, :] = jnp.zeros((ROWS, 8, C), jnp.float32)
    field[:, COLS + 8 : COLS + 16, :] = jnp.zeros((ROWS, 8, C), jnp.float32)
    field[:, 8 : COLS + 8, :] = latent_ref[0].astype(jnp.float32)
    for block in range(FRAMES):
        start = 6 + OWN * block
        piece = field[:, start : start + WIDE, :]
        out_ref[block] = piece.reshape(ROWS * WIDE, C).astype(jnp.bfloat16)


def pack(latent):
    return pl.pallas_call(
        pack_kernel,
        out_shape=jax.ShapeDtypeStruct((FRAMES, ROWS * WIDE, C), jnp.bfloat16),
        in_specs=[VMEM],
        out_specs=VMEM,
        scratch_shapes=[pltpu.VMEM((ROWS, COLS + 16, C), jnp.float32)],
        compiler_params=PARAMS,
    )(latent)


COUNT = ROWS * WIDE


def activate(value, gain_ref):
    return silu(norm_gain(value, gain_ref[...].reshape(1, 1, C)))


def time_taps(weight_ref, taps, times):
    return jnp.concatenate([weight_ref[time, taps, :] for time in times], 1)


def own_rows_kernel(streamed, main_ref, gain_ref, weight_ref, total_ref, field, stacked, *refs):
    if streamed:
        source, (weight_ref, arrived) = weight_ref, refs
        copies = []
        for time in range(3):
            for part in range(4):
                rows = pl.ds(part * 864, 864)
                copies.append(
                    pltpu.make_async_copy(
                        source.at[time, rows], weight_ref.at[time, rows], arrived.at[time, part]
                    )
                )
        for copy in copies:
            copy.start()
    field[:, :, WIDE:, :] = jnp.zeros((FRAMES, ROWS + 2, 8, C), jnp.float32)
    field[:, 0:1, 0:WIDE, :] = jnp.zeros((FRAMES, 1, WIDE, C), jnp.float32)
    field[:, ROWS + 1 :, 0:WIDE, :] = jnp.zeros((FRAMES, 1, WIDE, C), jnp.float32)

    for t in range(FRAMES):
        main = main_ref[t].astype(jnp.float32).reshape(ROWS, WIDE, C)
        field[t, 1 : ROWS + 1, 0:WIDE, :] = activate(main, gain_ref)
        for dh in range(3):
            for dw in range(3):
                piece = field[t, dh : dh + ROWS, dw : dw + WIDE, :]
                lanes = (dh * 3 + dw) * C
                stacked[t * COUNT : t * COUNT + COUNT, lanes : lanes + C] = piece.reshape(
                    COUNT, C
                ).astype(jnp.bfloat16)
    if streamed:
        for copy in copies[:4]:
            copy.wait()
        total_ref[: 2 * COUNT, :] = jnp.zeros((2 * COUNT, C), jnp.float32)
        total_ref[2 * COUNT :, :] = jnp.dot(
            stacked[: 6 * COUNT, :],
            time_taps(weight_ref, slice(0, 9 * C), (0,)),
            preferred_element_type=jnp.float32,
        )
        for copy in copies[4:]:
            copy.wait()
    pair = time_taps(weight_ref, slice(0, 9 * C), (2, 1))
    both = jnp.dot(stacked[...], pair, preferred_element_type=jnp.float32)
    if streamed:
        total_ref[...] += both[:, :C]
    else:
        total_ref[...] = both[:, :C]
    total_ref[COUNT:, :] += both[: 7 * COUNT, C:]
    if not streamed:
        total_ref[2 * COUNT :, :] += jnp.dot(
            stacked[: 6 * COUNT, :],
            time_taps(weight_ref, slice(0, 9 * C), (0,)),
            preferred_element_type=jnp.float32,
        )


def edge_rows_kernel(add, total_ref, above_ref, below_ref, gain_ref, weight_ref, *refs):
    if add:
        latent_ref, out_ref, field, stacked, edge, shifted, trimmed = refs
    else:
        first_ref, out_ref, field, stacked, edge = refs
        column = lax.broadcasted_iota(jnp.int32, (ROWS, WIDE, C), 1).reshape(COUNT, C)
        column = column + first_ref[0]
        inside = (column >= 0) & (column < COLS)
    for side, rows_ref in enumerate((above_ref, below_ref)):
        field[side, :, WIDE:, :] = jnp.zeros((FRAMES, 8, C), jnp.float32)
        field[side, :, 0:WIDE, :] = activate(rows_ref[...].astype(jnp.float32), gain_ref)
        for dw in range(3):
            piece = field[side, :, dw : dw + WIDE, :]
            stacked[side, :, dw * C : dw * C + C] = piece.reshape(FRAMES * WIDE, C).astype(
                jnp.bfloat16
            )
        taps = slice(side * 6 * C, side * 6 * C + 3 * C)
        weights = time_taps(weight_ref, taps, (2, 1, 0))
        three = jnp.dot(stacked[side], weights, preferred_element_type=jnp.float32)
        edge[side] = three[:, :C]
        edge[side, WIDE:, :] += three[: 7 * WIDE, C : 2 * C]
        edge[side, 2 * WIDE :, :] += three[: 6 * WIDE, 2 * C :]
    for t in range(FRAMES):
        value = total_ref[t * COUNT : t * COUNT + COUNT, :]
        rows = slice(t * WIDE, t * WIDE + WIDE)
        value = jnp.concatenate(
            [
                value[:WIDE] + edge[0, rows, :],
                value[WIDE : 3 * WIDE],
                value[3 * WIDE :] + edge[1, rows, :],
            ],
            0,
        )
        if not add:
            out_ref[t] = jnp.where(inside, value, 0.0).astype(jnp.bfloat16)
            continue
        shifted[:, 8 : WIDE + 8, :] = latent_ref[t].astype(jnp.float32).reshape(ROWS, WIDE, C)
        value = value.reshape(ROWS, WIDE, C)[:, :OWN, :] + shifted[:, 10 : OWN + 10, :]
        for row in range(ROWS):
            trimmed[row * OWN : row * OWN + OWN, :] = value[row]
        out_ref[t] = trimmed[...].astype(jnp.bfloat16)


def convolve(main, place, gain, weight, latent=None):
    add = latent is not None
    gain = gain.reshape(1, C)
    even, outermost, first_column = place
    above, below = row_halos(main, even, outermost)
    streamed = not add
    total = pl.pallas_call(
        functools.partial(own_rows_kernel, streamed),
        out_shape=jax.ShapeDtypeStruct((FRAMES * COUNT, C), jnp.float32),
        in_specs=[VMEM, VMEM, pl.BlockSpec(memory_space=pltpu.HBM) if streamed else VMEM],
        out_specs=VMEM,
        scratch_shapes=[
            pltpu.VMEM((FRAMES, ROWS + 2, WIDE + 8, C), jnp.float32),
            pltpu.VMEM((FRAMES * COUNT, 9 * C), jnp.bfloat16),
        ]
        + streamed * [pltpu.VMEM((3, 9 * C, C), jnp.bfloat16), pltpu.SemaphoreType.DMA((3, 4))],
        compiler_params=STREAM_PARAMS if streamed else CONV_PARAMS,
        cost_estimate=pl.CostEstimate(
            flops=2 * 768 * 27 * C * C, bytes_accessed=27 * C * C * 2, transcendentals=10**6
        ),
    )(main, gain, pltpu.with_memory_space_constraint(weight, pltpu.HBM) if streamed else weight)
    operands = [total, above, below, gain, weight, latent if add else first_column]
    scratch = [
        pltpu.VMEM((2, FRAMES, WIDE + 8, C), jnp.float32),
        pltpu.VMEM((2, FRAMES * WIDE, 3 * C), jnp.bfloat16),
        pltpu.VMEM((2, FRAMES * WIDE, C), jnp.float32),
    ]
    if add:
        scratch.append(pltpu.VMEM((ROWS, WIDE + 8, C), jnp.float32))
        scratch.append(pltpu.VMEM((POS, C), jnp.float32))
    return pl.pallas_call(
        functools.partial(edge_rows_kernel, add),
        out_shape=jax.ShapeDtypeStruct((FRAMES, POS if add else COUNT, C), jnp.bfloat16),
        in_specs=[VMEM] * 5 + [VMEM if add else pl.BlockSpec(memory_space=pltpu.SMEM)],
        out_specs=VMEM,
        scratch_shapes=scratch,
        compiler_params=CONV_PARAMS,
        cost_estimate=pl.CostEstimate(
            flops=2 * 384 * 9 * C * C, bytes_accessed=27 * C * C * 2, transcendentals=10**5
        ),
    )(*operands)


def attend_kernel(count, group, start, end, span, *refs):
    if start:
        rows_ref, query_weight_ref, key_weight_ref = refs[:3]
        refs = refs[3:]
        scale = math.log2(math.e) / math.sqrt(C)
        query = jnp.dot(
            rows_ref[...], query_weight_ref[...], preferred_element_type=jnp.float32
        ).astype(jnp.bfloat16)
        query = lax.dot_general(
            query, key_weight_ref[...], ROW_DOT, preferred_element_type=jnp.float32
        )
        query = (query * scale).astype(jnp.bfloat16)
        top = summed = acc = None
    else:
        query_ref, acc_in, top_in, sum_in = refs[:4]
        refs = refs[4:]
        query = query_ref[span, :]
        top, summed, acc = top_in[span, :1], sum_in[span, :1], acc_in[span, :]
    blocks, outs = refs[:count], refs[count:]
    parts = [
        block[first : first + TILE, :]
        for block in blocks
        for first in range(0, block.shape[0], TILE)
    ]
    keys = [
        parts[first] if group == 1 else jnp.concatenate(parts[first : first + group], 0)
        for first in range(0, len(parts), group)
    ]

    def score(key):
        return lax.dot_general(query, key, ROW_DOT, preferred_element_type=jnp.float32)

    following = score(keys[0])
    for index, key in enumerate(keys):
        scores = following
        if index + 1 < len(keys):
            following = score(keys[index + 1])
        ceiling = scores.max(-1, keepdims=True)
        if top is not None:
            ceiling = jnp.maximum(ceiling, top)
        weights = jnp.exp2(scores - ceiling)
        new_sum = weights.sum(-1, keepdims=True)
        new_acc = jnp.dot(weights.astype(jnp.bfloat16), key, preferred_element_type=jnp.float32)
        if top is not None:
            shrink = jnp.exp2(top - ceiling)
            new_sum = summed * shrink + new_sum
            new_acc = acc * shrink + new_acc
        top, summed, acc = ceiling, new_sum, new_acc
    if end:
        share_out, level_out = outs
        share_out[...] = (acc / summed).astype(jnp.bfloat16)
        level_out[...] = jnp.broadcast_to(top + jnp.log2(summed), level_out.shape)
        return
    if start:
        outs[0][...] = query
        outs = outs[1:]
    acc_out, top_out, sum_out = outs
    acc_out[...] = acc
    top_out[...] = jnp.broadcast_to(top, top_out.shape)
    sum_out[...] = jnp.broadcast_to(summed, sum_out.shape)


def attend(source, blocks, group=1, start=False, end=False, span=slice(0, TILE)):
    rows = span.stop - span.start
    keys = sum(block.shape[0] for block in blocks)
    operands = [*source, *blocks]
    bf16 = jax.ShapeDtypeStruct((rows, C), jnp.bfloat16)
    column = jax.ShapeDtypeStruct((rows, 128), jnp.float32)
    outs = (jax.ShapeDtypeStruct((rows, C), jnp.float32), column, column)
    if end:
        outs = (bf16, column)
    elif start:
        outs = (bf16, *outs)
    return pl.pallas_call(
        functools.partial(attend_kernel, len(blocks), group, start, end, span),
        out_shape=outs,
        in_specs=[VMEM] * len(operands),
        out_specs=tuple(VMEM for _ in outs),
        compiler_params=PARAMS,
        cost_estimate=pl.CostEstimate(
            flops=4 * rows * keys * C, bytes_accessed=2 * keys * C, transcendentals=rows * keys
        ),
    )(*operands)


def finish_kernel(
    acc_ref,
    top_ref,
    sum_ref,
    first_ref,
    second_ref,
    level_ref,
    state_ref,
    value_ref,
    outw_ref,
    out_ref,
    field,
):
    own = top_ref[:, :1] + jnp.log2(sum_ref[:, :1])
    other = level_ref[...]
    ceiling = jnp.maximum(own, other)
    own_part = jnp.exp2(own - ceiling)
    other_part = jnp.exp2(other - ceiling)
    shares = jnp.concatenate([first_ref[...], second_ref[...]], 0).astype(jnp.float32)
    mixed = acc_ref[...] * (own_part / sum_ref[:, :1]) + shares * other_part
    mixed = (mixed / (own_part + other_part)).astype(jnp.bfloat16)
    attended = jnp.dot(mixed, value_ref[...], preferred_element_type=jnp.float32)
    result = jnp.dot(
        attended.astype(jnp.bfloat16), outw_ref[...], preferred_element_type=jnp.float32
    ) + state_ref[...].astype(jnp.float32)
    for block in range(FRAMES):
        for row in range(ROWS):
            start = (block * ROWS + row) * OWN
            field[row, block * OWN : block * OWN + OWN, :] = result[start : start + OWN, :]
    out_ref[0] = field[...].astype(jnp.bfloat16)


def finish(state, first, second, level, flat, value_weight, out_weight):
    return pl.pallas_call(
        finish_kernel,
        out_shape=jax.ShapeDtypeStruct((1, ROWS, COLS, C), jnp.bfloat16),
        in_specs=[VMEM] * 9,
        out_specs=VMEM,
        scratch_shapes=[pltpu.VMEM((ROWS, COLS, C), jnp.float32)],
        compiler_params=PARAMS,
    )(*state, first, second, level, flat, value_weight, out_weight)


def row_halos(field, even, outermost):
    top, bottom = field[:, :WIDE, :], field[:, (ROWS - 1) * WIDE :, :]
    far = send(jnp.where(even, top, bottom), NEXT_CHIP)
    near = send(jnp.where(even, bottom, top), CORE)
    far = jnp.where(outermost, jnp.bfloat16(0), far)
    return jnp.where(even, far, near), jnp.where(even, near, far)


def body(
    latent,
    norm1_gain,
    conv1_weight,
    norm2_gain,
    conv2_weight,
    attn_gain,
    query_weight,
    key_weight,
    value_weight,
    out_weight,
):
    tile = lax.axis_index("tile")
    place = (
        tile % 2 == 0,
        (tile == 0) | (tile == 15),
        (OWN * lax.axis_index("frame") - 1).reshape(1),
    )
    latent, place = lax.optimization_barrier((latent, place))
    field, norm1_gain, norm2_gain = lax.optimization_barrier(
        (lax.all_to_all(pack(latent), "frame", 0, 0), norm1_gain, norm2_gain)
    )
    conv_one = convolve(field, place, norm1_gain, conv1_weight.reshape(3, 9 * C, C))
    hstate = convolve(
        conv_one, place, norm2_gain, conv2_weight.reshape(3, 9 * C, C), field
    )
    flat = lax.all_to_all(hstate, "frame", 0, 0).reshape(FRAMES * POS, C)
    flat, attn_gain, query_weight, key_weight, value_weight, out_weight = (
        lax.optimization_barrier(
            (flat, attn_gain, query_weight, key_weight, value_weight, out_weight)
        )
    )
    normed = norm_gain(flat.astype(jnp.float32), attn_gain).astype(jnp.bfloat16)
    half = TILE // 2
    low, high = normed[:half], normed[half:]
    behind_low = send(low, UP_X)
    ahead_high = send(high, DOWN_X)
    across = send(normed, OTHER_Z)
    mate = send(normed, CORE)
    normed, mate, low, high = lax.optimization_barrier((normed, mate, low, high))
    behind_high = send(high, UP_X)
    ahead_low = send(low, DOWN_X)
    own = attend([normed, query_weight, key_weight], [normed, mate], start=True)
    (behind_low, ahead_high, own) = lax.optimization_barrier((behind_low, ahead_high, own))
    far_low = send(behind_low, UP_X)
    far_high = send(ahead_high, DOWN_X)
    early = jnp.concatenate([behind_low, ahead_high], 0)
    own = [own[0], *attend(own, [early])]
    (behind_high, ahead_low, own) = lax.optimization_barrier((behind_high, ahead_low, own))
    late = jnp.concatenate([behind_high, ahead_low], 0)
    near_mate = send(jnp.concatenate([early, late], 0), CORE)
    other_query, *other = attend(
        [across, query_weight, key_weight], [mate, early, late], start=True
    )
    (far_low, far_high, other) = lax.optimization_barrier((far_low, far_high, other))
    far = jnp.concatenate([far_low, far_high], 0)
    far_mate = send(far, CORE)
    other = attend([other_query, *other], [near_mate])
    other = [other_query, *other]
    first, first_level = attend(other, [far, far_mate], end=True, span=slice(0, half))
    other, first, first_level = lax.optimization_barrier((other, first, first_level))
    first_back = send(first, OTHER_Z)
    second, second_level = attend(other, [far, far_mate], end=True, span=slice(half, TILE))
    second_back = send(second, OTHER_Z)
    level = jnp.concatenate([first_level[:, 0], second_level[:, 0]], 0)
    level_back = send(level, OTHER_Z)
    own = lax.optimization_barrier((own, second))[0]
    own = attend(own, [across, late, near_mate, far, far_mate], group=2)
    return finish(
        own, first_back, second_back, level_back.reshape(-1, 1), flat, value_weight, out_weight
    )


def solution(mesh):
    return jax.shard_map(
        body,
        mesh=mesh,
        in_specs=(P("frame", "tile", None, None), P(), P(), P(), P(), P(), P(), P(), P(), P()),
        out_specs=P("frame", "tile", None, None),
        check_vma=False,
    )
```
